32 devices in a mesh: pipe: 2 (over y), lat: 4 (over x, core), lon: 4 (over z).
Axes of the slice: x: 2, y: 2, z: 4, core: 2. Of those that a mesh axis runs over, the one named last changes fastest.
Arguments:
- field: bfloat16 [192, 64, 1024], P(None, 'lat', 'lon'), may hold values from -6 to 6
- conv_weight: bfloat16 [192, 1728], replicated, may hold values from -0.15625 to 0.15625
- conv_bias: float32 [192], replicated, may hold values from -3 to 3
- expand_weight: bfloat16 [768, 192], replicated, may hold values from -0.4375 to 0.4375
- expand_bias: float32 [768], replicated, may hold values from -3 to 3
- project_weight: bfloat16 [192, 768], replicated, may hold values from -0.21875 to 0.21875
- project_bias: float32 [192], replicated, may hold values from -3 to 3
- out_cotangent: bfloat16 [192, 32, 512], P(None, 'lat', 'lon'), may hold values from -6 to 6
- dropout_key: int32 [2], replicated, may hold values from 0 to 1073741823
Outputs:
- section_fields: bfloat16 [2, 192, 32, 512], P('pipe', None, 'lat', 'lon')
- conv_grad: float32 [192, 1728], replicated
- conv_bias_grad: float32 [192], replicated
- expand_grad: float32 [768, 192], replicated
- expand_bias_grad: float32 [768], replicated
- project_grad: float32 [192, 768], replicated
- project_bias_grad: float32 [192], replicated
The draws below stay inside these ranges and needn't reach their ends.
All inputs are finite; a program needn't handle non-finite values.
Results may differ from the reference program's by a relative error of at most 0.0056.
Values may be sent and summed in bfloat16 or wider, within the bound.
A program may use at most 64 MiB of HBM per device.

```python
import jax
import jax.numpy as jnp
from jax import lax

C = 192
F = 768
HL = 16
NLAT = 64
NLON = 1024
NLAT2 = 32
NLON2 = 512
N_LAT = 4


def levels(stream_key, dims, cuts, smallest, high):
    loudness = 1.0
    for dim, parts in cuts:
        heights = jax.random.uniform(jax.random.fold_in(jax.random.fold_in(stream_key, 6), dim), (parts,), jnp.float32, smallest / len(cuts), high / len(cuts))
        loudness = loudness * jnp.repeat(jnp.exp(heights), dims[dim] // parts).reshape((-1,) + (1,) * (len(dims) - 1 - dim))
    return loudness


def scatter_about(own_key, shape, spread, bound, split=(), kind=jnp.bfloat16):
    values = jax.random.normal(own_key, shape, jnp.float32) * spread
    if len(split) > 0:
        values = levels(own_key, shape, split, -0.22, 0.18) * values
    return jnp.clip(values, min=-bound, max=bound).astype(kind)


def setup_inputs(seed: int = 0) -> dict:
    key_list = jax.random.split(jax.random.key(seed), 10)
    return {
        "field": scatter_about(key_list[0], (C, NLAT, NLON), 1.0, 6.0, ((1, 4), (2, 4))),
        "conv_weight": scatter_about(key_list[1], (C, 9 * C), (9 * C) ** -0.5, 0.15625),
        "conv_bias": scatter_about(key_list[2], (C,), 0.5, 3.0, (), jnp.float32),
        "expand_weight": scatter_about(key_list[3], (F, C), C ** -0.5, 0.4375),
        "expand_bias": scatter_about(key_list[4], (F,), 0.5, 3.0, (), jnp.float32),
        "project_weight": scatter_about(key_list[5], (C, F), F ** -0.5, 0.21875),
        "project_bias": scatter_about(key_list[6], (C,), 0.5, 3.0, (), jnp.float32),
        "out_cotangent": scatter_about(key_list[7], (C, NLAT2, NLON2), 1.0, 6.0, ((1, 4), (2, 4))),
        "dropout_key": jax.random.randint(key_list[8], (2,), 0, 1073741824).astype(jnp.int32),
    }


MIXER_ONE = -2048144789
MIXER_TWO = -1028477387
GOLDEN_STEP = -1640531535
KEEP_LEVEL = 819
KEEP_SCALE = 1024.0 / 819.0
HIGHEST_MODE = lax.Precision.HIGHEST

def shifted(number, places):
    return lax.shift_right_logical(number, jnp.full_like(number, places))

def scramble(number):
    number = number ^ shifted(number, 16)
    number = number * jnp.int32(MIXER_ONE)
    number = number ^ shifted(number, 13)
    number = number * jnp.int32(MIXER_TWO)
    return number ^ shifted(number, 16)

def keep_mask(cell_index, dropout_key):
    salt = scramble(dropout_key[0] + scramble(dropout_key[1]))
    hashed = scramble(cell_index * jnp.int32(GOLDEN_STEP) + salt)
    bucket = jnp.bitwise_and(shifted(hashed, 8), jnp.int32(1023))
    return jnp.where(bucket < KEEP_LEVEL, jnp.float32(KEEP_SCALE), jnp.float32(0.0))

def gelu_slope(point, incoming):
    return jax.vjp(jax.nn.gelu, point)[1](incoming)[0]

def rounded(array):
    return lax.optimization_barrier(array.astype(jnp.bfloat16)).astype(jnp.float32)

def convolve(padded, kernel):
    return lax.conv_general_dilated(padded, kernel, (2, 2), 'VALID', dimension_numbers=('NCHW', 'OIHW', 'NCHW'), precision=HIGHEST_MODE)

def reference(field, conv_weight, conv_bias, expand_weight, expand_bias, project_weight, project_bias, out_cotangent, dropout_key):
    half_rows = HL // 2
    scale = float(NLAT2 * NLON2) ** (-0.5)
    kernel = conv_weight.astype(jnp.float32).reshape(C, 3, 3, C).transpose(0, 3, 1, 2)
    w_expand = expand_weight.astype(jnp.float32)
    w_project = project_weight.astype(jnp.float32)
    mirror_row = jnp.roll(field[:, :1, :], -(NLON // 2), axis=2)

    def band_step(carry, band):
        conv_acc, conv_bias_acc, expand_acc, expand_bias_acc, project_acc, project_bias_acc = carry
        start = band * HL
        rows_band = lax.dynamic_slice_in_dim(field, start, HL, 1)
        north = lax.dynamic_slice_in_dim(field, jnp.maximum(start - 1, 0), 1, 1)
        top_row = jnp.where(band == 0, mirror_row, north)
        extended = jnp.concatenate([top_row, rows_band], axis=1)
        padded = jnp.concatenate([extended[:, :, -1:], extended], axis=2).astype(jnp.float32)[None]
        pre = convolve(padded, kernel)[0].reshape(C, half_rows * NLON2) + conv_bias[:, None]
        row_ids = band * half_rows + jnp.arange(half_rows, dtype=jnp.int32)
        cell_ids = (row_ids[:, None] * NLON2 + jnp.arange(NLON2, dtype=jnp.int32)[None, :]).reshape(-1)
        keep = keep_mask(cell_ids, dropout_key)[None, :]
        encoded = (jax.nn.gelu(pre) * keep).astype(jnp.bfloat16)
        encoded_wide = lax.optimization_barrier(encoded).astype(jnp.float32)
        inner = jnp.dot(w_expand, encoded_wide, precision=HIGHEST_MODE) + expand_bias[:, None]
        activated = rounded(jax.nn.gelu(inner))
        processed = (encoded_wide + jnp.dot(w_project, activated, precision=HIGHEST_MODE) + project_bias[:, None]).astype(jnp.bfloat16)
        cot_rows = lax.dynamic_slice_in_dim(out_cotangent, band * half_rows, half_rows, 1).reshape(C, half_rows * NLON2)
        scaled = cot_rows.astype(jnp.float32) * scale
        cot_half = rounded(scaled)
        project_acc = project_acc + jnp.dot(cot_half, activated.T, precision=HIGHEST_MODE)
        project_bias_acc = project_bias_acc + lax.optimization_barrier(jnp.sum(scaled, axis=1))
        d_inner = gelu_slope(inner, jnp.dot(w_project.T, cot_half, precision=HIGHEST_MODE))
        d_inner_half = rounded(d_inner)
        expand_acc = expand_acc + jnp.dot(d_inner_half, encoded_wide.T, precision=HIGHEST_MODE)
        expand_bias_acc = expand_bias_acc + lax.optimization_barrier(jnp.sum(d_inner, axis=1))
        d_encoded = rounded(scaled + jnp.dot(w_expand.T, d_inner_half, precision=HIGHEST_MODE))
        d_pre = gelu_slope(pre, d_encoded * keep)
        d_pre_half = rounded(d_pre)
        kernel_grad = jax.vjp(lambda kern: convolve(padded, kern), kernel)[1](d_pre_half.reshape(1, C, half_rows, NLON2))[0]
        conv_acc = conv_acc + kernel_grad.transpose(0, 2, 3, 1).reshape(C, 9 * C)
        conv_bias_acc = conv_bias_acc + lax.optimization_barrier(jnp.sum(d_pre, axis=1))
        carry = (conv_acc, conv_bias_acc, expand_acc, expand_bias_acc, project_acc, project_bias_acc)
        return (carry, (encoded.reshape(C, half_rows, NLON2), processed.reshape(C, half_rows, NLON2)))
    start_carry = (jnp.zeros((C, 9 * C), jnp.float32), jnp.zeros((C,), jnp.float32), jnp.zeros((F, C), jnp.float32), jnp.zeros((F,), jnp.float32), jnp.zeros((C, F), jnp.float32), jnp.zeros((C,), jnp.float32))
    final, (encoded_all, processed_all) = lax.scan(band_step, start_carry, jnp.arange(N_LAT, dtype=jnp.int32))
    encoded_all = encoded_all.transpose(1, 0, 2, 3).reshape(C, NLAT2, NLON2)
    processed_all = processed_all.transpose(1, 0, 2, 3).reshape(C, NLAT2, NLON2)
    section_fields = jnp.stack([encoded_all, processed_all])
    return (section_fields, final[0], final[1], final[2], final[3], final[4], final[5])
```

```python
import functools

import jax
import jax.numpy as jnp
from jax import lax
from jax.experimental import pallas as pl
from jax.experimental.pallas import tpu as pltpu
from jax.sharding import PartitionSpec as P

MIXER_ONE = -2048144789
MIXER_TWO = -1028477387
GOLDEN_STEP = -1640531535
KEEP_LEVEL = 819
KEEP_SCALE = 1024.0 / 819.0
ROOT = 0.7978845608028654
CUBIC = 0.044715
MESH = pl.DeviceIdType.MESH
BF = jnp.bfloat16
F32 = jnp.float32


def passed_along(value, axis, steps):
    count = lax.axis_size(axis)
    pairs = [(source, (source + steps) % count) for source in range(count)]
    return lax.ppermute(value, axis, pairs)


def shifted_2(block, axis, distance):
    devices = range(lax.axis_size(axis))
    route = [(i - distance, i) for i in devices if i - distance in devices]
    return lax.ppermute(block, axis, route)


def shifted(number, places):
    return lax.shift_right_logical(number, jnp.full_like(number, places))


def scramble(number):
    number = number ^ shifted(number, 16)
    number = number * jnp.int32(MIXER_ONE)
    number = number ^ shifted(number, 13)
    number = number * jnp.int32(MIXER_TWO)
    return number ^ shifted(number, 16)


def gelu_both(x):
    square = x * x
    t = jnp.tanh(ROOT * (x + CUBIC * (square * x)))
    cdf = 0.5 * (1.0 + t)
    slope = cdf + (0.5 * ROOT) * x * (1.0 - t * t) * (1.0 + (3.0 * CUBIC) * square)
    return x * cdf, slope


def gelu_only(x):
    t = jnp.tanh(ROOT * (x + CUBIC * (x * x * x)))
    return x * (0.5 * (1.0 + t))


def dot(left, right, dims):
    return lax.dot_general(left, right, (dims, ((), ())), preferred_element_type=F32)


NN = ((1,), (0,))
NT = ((1,), (1,))
TN = ((0,), (0,))


def compute_kernel(
    rows,
    cols,
    total_rows,
    scale,
    salt_ref,
    xt,
    top,
    west,
    cw,
    cb,
    ew,
    eb,
    pw,
    pb,
    cot,
    field_out,
    payload,
    patches,
    enc_s,
    act_s,
    cot_s,
    di_s,
    dp_s,
):
    channels, taps = cw.shape
    hidden = ew.shape[0]
    cells = rows * cols
    pad_taps = patches.shape[0]
    is_encoder = lax.axis_index("pipe") == 0
    lon_cols = cols * lax.axis_size("lon")
    row_base = lax.axis_index("lat") * rows
    col_base = lax.axis_index("lon") * cols

    source = lax.broadcasted_iota(jnp.int32, (2 * cols, 3 * cols), 0)
    target = lax.broadcasted_iota(jnp.int32, (2 * cols, 3 * cols), 1)
    tap = target // cols
    wanted = 2 * (target - tap * cols) + tap - 1
    select = jnp.where(source == wanted, 1.0, 0.0).astype(BF)
    edge_row = lax.broadcasted_iota(jnp.int32, (128, cols), 0)
    edge_col = lax.broadcasted_iota(jnp.int32, (128, cols), 1)
    west_edge = west[...]
    for q in range(2 * rows + 1):
        line = top[...] if q == 0 else xt[q - 1]
        split = dot(line, select, NN)
        pick = jnp.where((edge_row == q) & (edge_col == 0), 1.0, 0.0).astype(BF)
        first = (split[:, :cols] + dot(west_edge, pick, NN)).astype(BF)
        parts = [first, split[:, cols : 2 * cols].astype(BF), split[:, 2 * cols :].astype(BF)]
        places = [(1, q // 2)] if q % 2 else [(a, q // 2 - a // 2) for a in (0, 2)]
        for a, r in places:
            if 0 <= r < rows:
                for b in range(3):
                    start = (3 * a + b) * channels
                    patches[start : start + channels, r * cols : (r + 1) * cols] = parts[b]
    patches[taps:, :] = jnp.zeros((pad_taps - taps, cells), BF)

    lanes = lax.broadcasted_iota(jnp.int32, (channels, 128), 1)
    salt = salt_ref[0]
    step = 2 * cols
    sums = [0.0, 0.0, 0.0]
    for j in range(cells // step):
        here = slice(j * step, (j + 1) * step)
        lane = lax.broadcasted_iota(jnp.int32, (1, step), 1)
        local_row = lane // cols
        cell = (row_base + 2 * j + local_row) * lon_cols + col_base + lane - local_row * cols
        hashed = scramble(cell * jnp.int32(GOLDEN_STEP) + salt)
        bucket = jnp.bitwise_and(shifted(hashed, 8), jnp.int32(1023))
        keep = jnp.where(bucket < KEEP_LEVEL, F32(KEEP_SCALE), F32(0.0))
        pre = dot(cw[...], patches[:taps, here], NN) + cb[...]
        value, pre_slope = gelu_both(pre)
        encoded = (value * keep).astype(BF)
        inner = dot(ew[...], encoded, NN) + eb[...]
        activated, slope = gelu_both(inner)
        activated = activated.astype(BF)
        scaled = jnp.concatenate([cot[2 * j], cot[2 * j + 1]], axis=1).astype(F32) * scale
        cot_half = scaled.astype(BF)
        d_inner = dot(pw[...], cot_half, TN) * slope
        d_half = d_inner.astype(BF)

        def encoder_part(sums=sums):
            field_out[2 * j] = encoded[:, :cols]
            field_out[2 * j + 1] = encoded[:, cols:]
            d_encoded = (scaled + dot(ew[...], d_half, TN)).astype(BF)
            d_pre = d_encoded.astype(F32) * keep * pre_slope
            dp_s[:, here] = d_pre.astype(BF)
            act_s[0:channels, j * 128 : j * 128 + 128] = jnp.sum(d_pre, axis=1, keepdims=True) + jnp.zeros(
                (channels, 128), F32
            )

        def processor_part():
            processed = (encoded.astype(F32) + dot(pw[...], activated, NN) + pb[...]).astype(BF)
            field_out[2 * j] = processed[:, :cols]
            field_out[2 * j + 1] = processed[:, cols:]
            enc_s[:, here] = encoded
            cot_s[:, here] = cot_half
            di_s[:hidden, here] = activated
            di_s[hidden:, here] = d_half
            bias = jnp.where(lanes == 0, jnp.sum(scaled, axis=1, keepdims=True), 0.0)
            total = jnp.sum(d_inner, axis=1, keepdims=True)
            for k in range(hidden // channels):
                bias = jnp.where(lanes == k + 1, total[k * channels : (k + 1) * channels], bias)
            act_s[0:channels, j * 128 : j * 128 + 128] = bias

        pl.when(is_encoder)(encoder_part)
        pl.when(jnp.logical_not(is_encoder))(processor_part)

    def bias_total():
        total = act_s[:, 0:128]
        for j in range(1, cells // step):
            total = total + act_s[:, j * 128 : j * 128 + 128]
        return total

    blocks = pad_taps // 128

    @pl.when(is_encoder)
    def _():
        for k in range(blocks):
            block = dot(dp_s[...], patches[k * 128 : (k + 1) * 128, :], NT)
            if k == blocks - 1:
                block = jnp.where(lanes == taps - k * 128, bias_total(), block)
            payload[k * channels : (k + 1) * channels, :] = block.astype(BF)

    @pl.when(jnp.logical_not(is_encoder))
    def _():
        per = hidden // 128
        for k in range(per):
            block = dot(cot_s[...], di_s[k * 128 : (k + 1) * 128, :], NT)
            payload[k * channels : (k + 1) * channels, :] = block.astype(BF)
        for k in range(per):
            block = dot(enc_s[...], di_s[hidden + k * 128 : hidden + (k + 1) * 128, :], NT)
            payload[(per + k) * channels : (per + k + 1) * channels, :] = block.astype(BF)
        payload[2 * per * channels : (2 * per + 1) * channels, :] = bias_total().astype(BF)
        rest = (2 * per + 1) * channels
        payload[rest : blocks * channels, :] = jnp.zeros((blocks * channels - rest, 128), BF)

    payload[blocks * channels :, :] = jnp.zeros((total_rows - blocks * channels, 128), BF)


def reduce_kernel(
    n_x, n_z, payload, out, buf1, s1, buf2, s2, buf3, send, recv
):
    pipe = lax.axis_index("pipe")
    lat = lax.axis_index("lat")
    z = lax.axis_index("lon")
    x = lat // 2
    core = lat % 2
    total_rows = payload.shape[0]
    half = total_rows // 2
    part = half // n_x
    own = part // n_z
    twin = (pipe, 2 * x + 1 - core, z)

    def z_peer(d):
        return (pipe, lat, (z + d) % n_z)

    def xp_peer(dx, dp):
        return ((pipe + dp) % 2, 2 * ((x + dx) % n_x) + core, z)

    others = [(dx, dp) for dp in range(2) for dx in range(n_x) if dx or dp]
    peers = [twin] + [z_peer(d) for d in range(1, n_z)] + [xp_peer(*o) for o in others]
    barrier = pltpu.get_barrier_semaphore()
    for peer in peers:
        pl.semaphore_signal(barrier, inc=1, device_id=peer, device_id_type=MESH)
    pl.semaphore_wait(barrier, len(peers))

    count = [0]
    started = []

    def push(src, dst, peer):
        i = count[0]
        count[0] += 1
        copy = pltpu.make_async_remote_copy(
            src_ref=src,
            dst_ref=dst,
            send_sem=send.at[i],
            recv_sem=recv.at[i],
            device_id=peer,
            device_id_type=MESH,
        )
        copy.start()
        started.append(copy)
        return copy

    def at(start, size):
        return pl.ds(pl.multiple_of(start, 16), size)

    push(payload.at[at((1 - core) * half, half)], buf1, twin).wait_recv()
    s1[...] = (payload[at(core * half, half), :].astype(F32) + buf1[...].astype(F32)).astype(BF)

    arrivals = []
    for d in range(1, n_x):
        arrivals.append(push(s1.at[at(((x + d) % n_x) * part, part)], buf2.at[d - 1], xp_peer(d, 0)))
    total = s1[at(x * part, part), :].astype(F32)
    for d in range(1, n_x):
        arrivals[d - 1].wait_recv()
        total = total + buf2[d - 1].astype(F32)
    s2[...] = total.astype(BF)

    arrivals = []
    for d in range(1, n_z):
        arrivals.append(push(s2.at[at(((z + d) % n_z) * own, own)], buf3.at[d - 1], z_peer(d)))
    total = s2[at(z * own, own), :].astype(F32)
    for d in range(1, n_z):
        arrivals[d - 1].wait_recv()
        total = total + buf3[d - 1].astype(F32)
    mine = out.at[pipe, at(core * half + x * part + z * own, own)]
    mine[...] = total.astype(BF)

    arrivals = [push(mine, mine, z_peer(d)) for d in range(1, n_z)]
    for copy in arrivals:
        copy.wait_recv()
    column = out.at[pipe, at(core * half + x * part, part)]
    arrivals = [push(column, column, xp_peer(*o)) for o in others]
    final = [push(column, column, twin)]
    for (dx, dp), copy in zip(others, arrivals):
        copy.wait_recv()
        block = out.at[(pipe + dp) % 2, at(core * half + ((x - dx + n_x) % n_x) * part, part)]
        final.append(push(block, block, twin))
    for copy in final:
        copy.wait_recv()
    for copy in started:
        copy.wait_send()


def per_device(
    field,
    conv_weight,
    conv_bias,
    expand_weight,
    expand_bias,
    project_weight,
    project_bias,
    out_cotangent,
    dropout_key,
):
    channels, row_count, col_count = field.shape
    hidden = expand_weight.shape[0]
    taps = conv_weight.shape[1]
    rows = row_count // 2
    cols = col_count // 2
    cells = rows * cols
    n_lat = lax.axis_size("lat")
    n_lon = lax.axis_size("lon")
    scale = float(cells * n_lat * n_lon) ** (-0.5)

    from_above = shifted_2(field[:, row_count - 1, :], "lat", 1)
    mirrored = passed_along(field[:, 0, :], "lon", n_lon // 2)
    top = jnp.where(lax.axis_index("lat") == 0, mirrored, from_above)
    edge = jnp.concatenate([top[:, col_count - 1 :], field[:, :, col_count - 1]], axis=1)
    west = passed_along(edge, "lon", 1)
    west = jnp.pad(west, ((0, 0), (0, 128 - row_count - 1)))
    salt = scramble(dropout_key[0] + scramble(dropout_key[1])).reshape(1)

    pad_taps = -(-(taps + 1) // 128) * 128
    blocks = pad_taps // 128
    unit = 16 * n_lat * n_lon
    total_rows = -(-(blocks * channels) // unit) * unit
    vmem = pl.BlockSpec(memory_space=pltpu.VMEM)
    smem = pl.BlockSpec(memory_space=pltpu.SMEM)
    field_out, payload = pl.pallas_call(
        functools.partial(compute_kernel, rows, cols, total_rows, scale),
        out_shape=(
            jax.ShapeDtypeStruct((rows, channels, cols), BF),
            jax.ShapeDtypeStruct((total_rows, 128), BF),
        ),
        in_specs=[smem] + [vmem] * 10,
        out_specs=(vmem, vmem),
        scratch_shapes=[
            pltpu.VMEM((pad_taps, cells), BF),
            pltpu.VMEM((channels, cells), BF),
            pltpu.VMEM((channels, cells // (2 * cols) * 128), F32),
            pltpu.VMEM((channels, cells), BF),
            pltpu.VMEM((2 * hidden, cells), BF),
            pltpu.VMEM((channels, cells), BF),
        ],
        compiler_params=pltpu.CompilerParams(vmem_limit_bytes=40 * 1024 * 1024),
        name="segment",
    )(
        salt,
        jnp.transpose(field, (1, 0, 2)),
        top,
        west,
        conv_weight,
        conv_bias[:, None],
        expand_weight,
        expand_bias[:, None],
        project_weight,
        project_bias[:, None],
        jnp.transpose(out_cotangent, (1, 0, 2)),
    )

    n_x = n_lat // 2
    half = total_rows // 2
    part = half // n_x
    own = part // n_lon
    copies = 1 + (n_x - 1) + 2 * (n_lon - 1) + 2 * (2 * n_x - 1) + 1
    gathered = pl.pallas_call(
        functools.partial(reduce_kernel, n_x, n_lon),
        out_shape=jax.ShapeDtypeStruct((2, total_rows, 128), BF),
        in_specs=[vmem],
        out_specs=vmem,
        scratch_shapes=[
            pltpu.VMEM((half, 128), BF),
            pltpu.VMEM((half, 128), BF),
            pltpu.VMEM((n_x - 1, part, 128), BF),
            pltpu.VMEM((part, 128), BF),
            pltpu.VMEM((n_lon - 1, own, 128), BF),
            pltpu.SemaphoreType.DMA((copies,)),
            pltpu.SemaphoreType.DMA((copies,)),
        ],
        compiler_params=pltpu.CompilerParams(
            collective_id=0, has_side_effects=True, vmem_limit_bytes=40 * 1024 * 1024
        ),
        name="gradient_sum",
    )(payload)

    used = gathered[:, : blocks * channels].reshape(2, blocks, channels, 128)
    wide = used[0].transpose(1, 0, 2).reshape(channels, pad_taps).astype(F32)
    conv_grad = wide[:, :taps]
    conv_bias_grad = wide[:, taps]
    per = hidden // 128
    project_grad = used[1, :per].transpose(1, 0, 2).reshape(channels, hidden).astype(F32)
    expand_grad = used[1, per : 2 * per].transpose(0, 2, 1).reshape(hidden, channels).astype(F32)
    biases = used[1, 2 * per].astype(F32)
    project_bias_grad = biases[:, 0]
    expand_bias_grad = biases[:, 1 : 1 + hidden // channels].T.reshape(hidden)
    section_fields = jnp.transpose(field_out, (1, 0, 2))[None]
    return (
        section_fields,
        conv_grad,
        conv_bias_grad,
        expand_grad,
        expand_bias_grad,
        project_grad,
        project_bias_grad,
    )


def solution(mesh):
    placed = (P(None, "lat", "lon"), P(), P(), P(), P(), P(), P(), P(None, "lat", "lon"), P())
    return jax.shard_map(
        per_device,
        mesh=mesh,
        in_specs=placed,
        out_specs=(P("pipe", None, "lat", "lon"), P(), P(), P(), P(), P(), P()),
        check_vma=False,
    )
```

```python
import functools

import jax
import jax.numpy as jnp
from jax import lax
from jax.experimental import pallas as pl
from jax.experimental.pallas import tpu as pltpu
from jax.sharding import PartitionSpec as P

MIXER_ONE = -2048144789
MIXER_TWO = -1028477387
GOLDEN_STEP = -1640531535
KEEP_LEVEL = 819
KEEP_SCALE = 1024.0 / 819.0
ROOT = 0.7978845608028654
CUBIC = 0.044715
MESH = pl.DeviceIdType.MESH
FLOWS = 3
BF = jnp.bfloat16
F32 = jnp.float32


def shifted(number, places):
    return lax.shift_right_logical(number, jnp.full_like(number, places))


def scramble(number):
    number = number ^ shifted(number, 16)
    number = number * jnp.int32(MIXER_ONE)
    number = number ^ shifted(number, 13)
    number = number * jnp.int32(MIXER_TWO)
    return number ^ shifted(number, 16)


def gelu_both(x):
    square = x * x
    t = jnp.tanh(ROOT * (x + CUBIC * (square * x)))
    cdf = 0.5 * (1.0 + t)
    slope = cdf + (0.5 * ROOT) * x * (1.0 - t * t) * (1.0 + (3.0 * CUBIC) * square)
    return x * cdf, slope


def gelu_only(x):
    t = jnp.tanh(ROOT * (x + CUBIC * (x * x * x)))
    return x * (0.5 * (1.0 + t))


def dot(left, right, dims):
    return lax.dot_general(left, right, (dims, ((), ())), preferred_element_type=F32)


NN = ((1,), (0,))
NT = ((1,), (1,))
TN = ((0,), (0,))


def compute_kernel(
    rows,
    cols,
    total_rows,
    scale,
    salt_ref,
    xt,
    top,
    west,
    corner,
    cw,
    cb,
    ew,
    eb,
    pw,
    pb,
    cot,
    field_out,
    payload,
    patches,
    enc_s,
    act_s,
    cot_s,
    di_s,
    dp_s,
):
    channels, taps = cw.shape
    hidden = ew.shape[1]
    cells = rows * cols
    pad_taps = patches.shape[0]
    is_encoder = lax.axis_index("pipe") == 0
    lon_cols = cols * lax.axis_size("lon")
    row_base = lax.axis_index("lat") * rows
    col_base = lax.axis_index("lon") * cols

    source = lax.broadcasted_iota(jnp.int32, (2 * cols, 3 * cols), 0)
    target = lax.broadcasted_iota(jnp.int32, (2 * cols, 3 * cols), 1)
    tap = target // cols
    wanted = 2 * (target - tap * cols) + tap - 1
    select = jnp.where(source == wanted, 1.0, 0.0).astype(BF)
    edge_row = lax.broadcasted_iota(jnp.int32, (128, cols), 0)
    edge_col = lax.broadcasted_iota(jnp.int32, (128, cols), 1)
    for q in range(2 * rows + 1):
        line = top[...] if q == 0 else xt[q - 1]
        split = dot(line, select, NN)
        lane = 127 if q == 0 else q - 1
        edge = corner[...] if q == 0 else west[...]
        pick = jnp.where((edge_row == lane) & (edge_col == 0), 1.0, 0.0).astype(BF)
        first = (split[:, :cols] + dot(edge, pick, NN)).astype(BF)
        parts = [first, split[:, cols : 2 * cols].astype(BF), split[:, 2 * cols :].astype(BF)]
        places = [(1, q // 2)] if q % 2 else [(a, q // 2 - a // 2) for a in (0, 2)]
        for a, r in places:
            if 0 <= r < rows:
                for b in range(3):
                    start = (3 * a + b) * channels
                    patches[start : start + channels, r * cols : (r + 1) * cols] = parts[b]
    patches[taps:, :] = jnp.zeros((pad_taps - taps, cells), BF)

    lanes = lax.broadcasted_iota(jnp.int32, (channels, 128), 1)
    salt = salt_ref[0]
    step = 2 * cols
    sums = [0.0, 0.0, 0.0]
    for j in range(cells // step):
        here = slice(j * step, (j + 1) * step)
        lane = lax.broadcasted_iota(jnp.int32, (1, step), 1)
        local_row = lane // cols
        cell = (row_base + 2 * j + local_row) * lon_cols + col_base + lane - local_row * cols
        hashed = scramble(cell * jnp.int32(GOLDEN_STEP) + salt)
        bucket = jnp.bitwise_and(shifted(hashed, 8), jnp.int32(1023))
        keep = jnp.where(bucket < KEEP_LEVEL, F32(KEEP_SCALE), F32(0.0))
        pre = dot(cw[...], patches[:taps, here], NN) + cb[...]
        value, pre_slope = gelu_both(pre)
        encoded = (value * keep).astype(BF)
        inner = dot(ew[...], encoded, TN) + eb[...]
        activated, slope = gelu_both(inner)
        activated = activated.astype(BF)
        scaled = jnp.concatenate([cot[2 * j], cot[2 * j + 1]], axis=1).astype(F32) * scale
        cot_half = scaled.astype(BF)
        d_inner = dot(pw[...], cot_half, TN) * slope
        d_half = d_inner.astype(BF)

        def encoder_part(sums=sums):
            field_out[2 * j] = encoded[:, :cols]
            field_out[2 * j + 1] = encoded[:, cols:]
            d_encoded = (scaled + dot(ew[...], d_half, NN)).astype(BF)
            d_pre = d_encoded.astype(F32) * keep * pre_slope
            dp_s[:, here] = d_pre.astype(BF)
            act_s[0:channels, j * 128 : j * 128 + 128] = jnp.sum(d_pre, axis=1, keepdims=True) + jnp.zeros(
                (channels, 128), F32
            )

        def processor_part():
            processed = (encoded.astype(F32) + dot(pw[...], activated, NN) + pb[...]).astype(BF)
            field_out[2 * j] = processed[:, :cols]
            field_out[2 * j + 1] = processed[:, cols:]
            enc_s[:, here] = encoded
            cot_s[:, here] = cot_half
            di_s[:hidden, here] = activated
            di_s[hidden:, here] = d_half
            bias = jnp.where(lanes == 0, jnp.sum(scaled, axis=1, keepdims=True), 0.0)
            total = jnp.sum(d_inner, axis=1, keepdims=True)
            for k in range(hidden // channels):
                bias = jnp.where(lanes == k + 1, total[k * channels : (k + 1) * channels], bias)
            act_s[0:channels, j * 128 : j * 128 + 128] = bias

        pl.when(is_encoder)(encoder_part)
        pl.when(jnp.logical_not(is_encoder))(processor_part)

    def bias_total():
        total = act_s[:, 0:128]
        for j in range(1, cells // step):
            total = total + act_s[:, j * 128 : j * 128 + 128]
        return total

    blocks = pad_taps // 128

    @pl.when(is_encoder)
    def _():
        for k in range(blocks):
            block = dot(dp_s[...], patches[k * 128 : (k + 1) * 128, :], NT)
            if k == blocks - 1:
                block = jnp.where(lanes == taps - k * 128, bias_total(), block)
            payload[k * channels : (k + 1) * channels, :] = block.astype(BF)

    @pl.when(jnp.logical_not(is_encoder))
    def _():
        per = hidden // 128
        for k in range(per):
            block = dot(cot_s[...], di_s[k * 128 : (k + 1) * 128, :], NT)
            payload[k * channels : (k + 1) * channels, :] = block.astype(BF)
        for k in range(per):
            block = dot(enc_s[...], di_s[hidden + k * 128 : hidden + (k + 1) * 128, :], NT)
            payload[(per + k) * channels : (per + k + 1) * channels, :] = block.astype(BF)
        payload[2 * per * channels : (2 * per + 1) * channels, :] = bias_total().astype(BF)
        rest = (2 * per + 1) * channels
        payload[rest : blocks * channels, :] = jnp.zeros((blocks * channels - rest, 128), BF)

    payload[blocks * channels :, :] = jnp.zeros((total_rows - blocks * channels, 128), BF)


def halo_kernel(n_lat, n_lon, xt, top, west, corner, edge, send, recv):
    pipe = lax.axis_index("pipe")
    lat = lax.axis_index("lat")
    lon = lax.axis_index("lon")
    last = xt.shape[0] - 1
    width = xt.shape[2]
    away = n_lon // 2
    is_first = lat == 0
    north = jnp.where(is_first, 0, lat - 1)
    turn = jnp.where(is_first, away, 0)
    has_south = lat < n_lat - 1
    sources = [
        (pipe, lat, (lon + n_lon - 1) % n_lon),
        (pipe, north, (lon + n_lon - turn) % n_lon),
        (pipe, north, (lon + n_lon - turn - 1 + n_lon) % n_lon),
    ]
    barrier = pltpu.get_barrier_semaphore()
    for peer in sources:
        pl.semaphore_signal(barrier, inc=1, device_id=peer, device_id_type=MESH)
    sends = 1 + jnp.where(has_south, 2, 0) + jnp.where(is_first, 2, 0)

    def copy(src, dst, i, j, peer):
        return pltpu.make_async_remote_copy(
            src_ref=src,
            dst_ref=dst,
            send_sem=send.at[i],
            recv_sem=recv.at[j],
            device_id=peer,
            device_id_type=MESH,
        )

    right = pl.ds(width - 128, 128)

    def pair(row, i, lat_to, lon_to):
        return [
            copy(xt.at[row], top, i, 0, (pipe, lat_to, lon_to % n_lon)),
            copy(xt.at[row, :, right], corner, i + 1, 1, (pipe, lat_to, (lon_to + 1) % n_lon)),
        ]

    south = pair(last, 0, jnp.where(has_south, lat + 1, lat), lon)
    pole = pair(0, 2, lat, lon + away)
    pl.semaphore_wait(barrier, sends)

    @pl.when(has_south)
    def _():
        for item in south:
            item.start()

    @pl.when(is_first)
    def _():
        for item in pole:
            item.start()

    row_id = lax.broadcasted_iota(jnp.int32, (128, 128), 0)
    col_id = lax.broadcasted_iota(jnp.int32, (128, 128), 1)
    total = None
    for q in range(last + 1):
        pick = jnp.where((row_id == 127) & (col_id == q), 1.0, 0.0).astype(BF)
        term = dot(xt[q, :, width - 128 :], pick, NN)
        total = term if total is None else total + term
    edge[...] = total.astype(BF)
    east = copy(edge, west, 4, 2, (pipe, lat, (lon + 1) % n_lon))
    east.start()
    for item in pole:
        item.wait_recv()
    east.wait()

    @pl.when(has_south)
    def _():
        for item in south:
            item.wait_send()

    @pl.when(is_first)
    def _():
        for item in pole:
            item.wait_send()


def finish_kernel(taps, hidden, gathered, conv, project, expand, conv_bias, biases):
    channels = conv.shape[0]
    blocks = -(-(taps + 1) // 128)
    per = hidden // 128
    for k in range(blocks):
        width = min(128, taps - 128 * k)
        block = gathered[0, k * channels : (k + 1) * channels, :]
        conv[:, 128 * k : 128 * k + width] = block[:, :width].astype(F32)
        if k == blocks - 1:
            pick = lax.broadcasted_iota(jnp.int32, (8, 128), 1) == taps - 128 * k
            conv_bias[...] = dot(jnp.where(pick, 1.0, 0.0).astype(BF), block, NT)
    for k in range(per):
        here = slice(128 * k, 128 * k + 128)
        project[:, here] = gathered[1, k * channels : (k + 1) * channels, :].astype(F32)
        expand[:, here] = gathered[1, (per + k) * channels : (per + k + 1) * channels, :].astype(F32)
    block = gathered[1, 2 * per * channels : (2 * per + 1) * channels, :]
    pick = lax.broadcasted_iota(jnp.int32, (8, 128), 1) == lax.broadcasted_iota(jnp.int32, (8, 128), 0)
    biases[...] = dot(jnp.where(pick, 1.0, 0.0).astype(BF), block, NT)


def reduce_kernel(n_x, n_z, flows, payload, out, buf1, s1, buf2, s2, buf3, send, recv):
    pipe = lax.axis_index("pipe")
    lat = lax.axis_index("lat")
    z = lax.axis_index("lon")
    x = lat // 2
    core = lat % 2
    twin = (pipe, 2 * x + 1 - core, z)

    def z_peer(d):
        return (pipe, lat, (z + d) % n_z)

    def xp_peer(dx, dp):
        return ((pipe + dp) % 2, 2 * ((x + dx) % n_x) + core, z)

    others = [(dx, dp) for dp in range(2) for dx in range(n_x) if dx or dp]
    peers = [twin] + [z_peer(d) for d in range(1, n_z)] + [xp_peer(*o) for o in others]
    barrier = pltpu.get_barrier_semaphore()
    for peer in peers:
        pl.semaphore_signal(barrier, inc=1, device_id=peer, device_id_type=MESH)
    pl.semaphore_wait(barrier, len(peers))

    count = [0]
    started = []

    def push(src, dst, peer):
        i = count[0]
        count[0] += 1
        copy = pltpu.make_async_remote_copy(
            src_ref=src,
            dst_ref=dst,
            send_sem=send.at[i],
            recv_sem=recv.at[i],
            device_id=peer,
            device_id_type=MESH,
        )
        copy.start()
        started.append(copy)
        return copy

    def at(start, size):
        return pl.ds(pl.multiple_of(start, 16), size)

    halves = [size // 2 for _, size in flows]
    parts = [half // n_x for half in halves]
    owns = [part // n_z for part in parts]
    ids = range(len(flows))

    firsts = []
    for f in ids:
        start = flows[f][0]
        half = halves[f]
        source = payload.at[at(start + (1 - core) * half, half)]
        firsts.append(push(source, buf1.at[f, pl.ds(0, half)], twin))

    seconds = []
    for f in ids:
        half, part = halves[f], parts[f]
        firsts[f].wait_recv()
        kept = payload[at(flows[f][0] + core * half, half), :]
        s1[f, :half] = (kept.astype(F32) + buf1[f, :half].astype(F32)).astype(BF)
        seconds.append(
            [
                push(
                    s1.at[f, at(((x + d) % n_x) * part, part)],
                    buf2.at[f, d - 1, pl.ds(0, part)],
                    xp_peer(d, 0),
                )
                for d in range(1, n_x)
            ]
        )

    thirds = []
    for f in ids:
        part, own = parts[f], owns[f]
        total = s1[f, at(x * part, part), :].astype(F32)
        for d in range(1, n_x):
            seconds[f][d - 1].wait_recv()
            total = total + buf2[f, d - 1, :part].astype(F32)
        s2[f, :part] = total.astype(BF)
        thirds.append(
            [
                push(
                    s2.at[f, at(((z + d) % n_z) * own, own)],
                    buf3.at[f, d - 1, pl.ds(0, own)],
                    z_peer(d),
                )
                for d in range(1, n_z)
            ]
        )

    fourths = []
    for f in ids:
        part, own = parts[f], owns[f]
        total = s2[f, at(z * own, own), :].astype(F32)
        for d in range(1, n_z):
            thirds[f][d - 1].wait_recv()
            total = total + buf3[f, d - 1, :own].astype(F32)
        place = at(flows[f][0] + core * halves[f] + x * part + z * own, own)
        mine = out.at[pipe, place]
        mine[...] = total.astype(BF)
        fourths.append([push(mine, mine, z_peer(d)) for d in range(1, n_z)])

    fifths = []
    final = []
    for f in ids:
        for copy in fourths[f]:
            copy.wait_recv()
        column = out.at[pipe, at(flows[f][0] + core * halves[f] + x * parts[f], parts[f])]
        fifths.append([push(column, column, xp_peer(*o)) for o in others])
        final.append(push(column, column, twin))
    for f in ids:
        for (dx, dp), copy in zip(others, fifths[f]):
            copy.wait_recv()
            start = flows[f][0] + core * halves[f] + ((x - dx + n_x) % n_x) * parts[f]
            block = out.at[(pipe + dp) % 2, at(start, parts[f])]
            final.append(push(block, block, twin))
    for copy in final:
        copy.wait_recv()
    for copy in started:
        copy.wait_send()


def per_device(
    field,
    conv_weight,
    conv_bias,
    expand_weight,
    expand_bias,
    project_weight,
    project_bias,
    out_cotangent,
    dropout_key,
):
    channels, row_count, col_count = field.shape
    hidden = expand_weight.shape[0]
    taps = conv_weight.shape[1]
    rows = row_count // 2
    cols = col_count // 2
    cells = rows * cols
    n_lat = lax.axis_size("lat")
    n_lon = lax.axis_size("lon")
    scale = float(cells * n_lat * n_lon) ** (-0.5)

    salt = scramble(dropout_key[0] + scramble(dropout_key[1])).reshape(1)

    pad_taps = -(-(taps + 1) // 128) * 128
    blocks = pad_taps // 128
    unit = 16 * n_lat * n_lon
    total_rows = -(-(blocks * channels) // unit) * unit
    vmem = pl.BlockSpec(memory_space=pltpu.VMEM)
    smem = pl.BlockSpec(memory_space=pltpu.SMEM)
    turned = jnp.transpose(field, (1, 0, 2))
    row_shape = jax.ShapeDtypeStruct((channels, col_count), BF)
    edge_shape = jax.ShapeDtypeStruct((channels, 128), BF)
    top, west, corner = pl.pallas_call(
        functools.partial(halo_kernel, n_lat, n_lon),
        out_shape=(row_shape, edge_shape, edge_shape),
        in_specs=[vmem],
        out_specs=(vmem, vmem, vmem),
        scratch_shapes=[
            pltpu.VMEM((channels, 128), BF),
            pltpu.SemaphoreType.DMA((5,)),
            pltpu.SemaphoreType.DMA((3,)),
        ],
        compiler_params=pltpu.CompilerParams(
            collective_id=1, has_side_effects=True, vmem_limit_bytes=16 * 1024 * 1024
        ),
        name="halo",
    )(turned)
    field_out, payload = pl.pallas_call(
        functools.partial(compute_kernel, rows, cols, total_rows, scale),
        out_shape=(
            jax.ShapeDtypeStruct((rows, channels, cols), BF),
            jax.ShapeDtypeStruct((total_rows, 128), BF),
        ),
        in_specs=[smem] + [vmem] * 11,
        out_specs=(vmem, vmem),
        scratch_shapes=[
            pltpu.VMEM((pad_taps, cells), BF),
            pltpu.VMEM((channels, cells), BF),
            pltpu.VMEM((channels, cells // (2 * cols) * 128), F32),
            pltpu.VMEM((channels, cells), BF),
            pltpu.VMEM((2 * hidden, cells), BF),
            pltpu.VMEM((channels, cells), BF),
        ],
        compiler_params=pltpu.CompilerParams(vmem_limit_bytes=40 * 1024 * 1024),
        name="segment",
    )(
        salt,
        turned,
        top,
        west,
        corner,
        conv_weight,
        conv_bias[:, None],
        expand_weight.T,
        expand_bias[:, None],
        project_weight,
        project_bias[:, None],
        jnp.transpose(out_cotangent, (1, 0, 2)),
    )

    n_x = n_lat // 2
    units = total_rows // unit
    count = min(FLOWS, units)
    sizes = [(units // count + (1 if f < units % count else 0)) * unit for f in range(count)]
    flows = [(sum(sizes[:f]), sizes[f]) for f in range(count)]
    half = sizes[0] // 2
    part = half // n_x
    own = part // n_lon
    copies = count * (1 + (n_x - 1) + 2 * (n_lon - 1) + 2 * (2 * n_x - 1) + 1)
    gathered = pl.pallas_call(
        functools.partial(reduce_kernel, n_x, n_lon, flows),
        out_shape=jax.ShapeDtypeStruct((2, total_rows, 128), BF),
        in_specs=[vmem],
        out_specs=vmem,
        scratch_shapes=[
            pltpu.VMEM((count, half, 128), BF),
            pltpu.VMEM((count, half, 128), BF),
            pltpu.VMEM((count, n_x - 1, part, 128), BF),
            pltpu.VMEM((count, part, 128), BF),
            pltpu.VMEM((count, n_lon - 1, own, 128), BF),
            pltpu.SemaphoreType.DMA((copies,)),
            pltpu.SemaphoreType.DMA((copies,)),
        ],
        compiler_params=pltpu.CompilerParams(
            collective_id=0, has_side_effects=True, vmem_limit_bytes=40 * 1024 * 1024
        ),
        name="gradient_sum",
    )(payload)

    wide = jax.ShapeDtypeStruct((channels, hidden), F32)
    short = jax.ShapeDtypeStruct((8, channels), F32)
    conv_grad, project_grad, expand_turned, conv_rows, bias_rows = pl.pallas_call(
        functools.partial(finish_kernel, taps, hidden),
        out_shape=(jax.ShapeDtypeStruct((channels, taps), F32), wide, wide, short, short),
        in_specs=[vmem],
        out_specs=(vmem,) * 5,
        compiler_params=pltpu.CompilerParams(vmem_limit_bytes=32 * 1024 * 1024),
        name="widen",
    )(gathered)
    expand_grad = expand_turned.T
    conv_bias_grad = conv_rows[0]
    project_bias_grad = bias_rows[0]
    expand_bias_grad = bias_rows[1 : 1 + hidden // channels].reshape(hidden)
    section_fields = jnp.transpose(field_out, (1, 0, 2))[None]
    return (
        section_fields,
        conv_grad,
        conv_bias_grad,
        expand_grad,
        expand_bias_grad,
        project_grad,
        project_bias_grad,
    )


def solution(mesh):
    placed = (P(None, "lat", "lon"), P(), P(), P(), P(), P(), P(), P(None, "lat", "lon"), P())
    return jax.shard_map(
        per_device,
        mesh=mesh,
        in_specs=placed,
        out_specs=(P("pipe", None, "lat", "lon"), P(), P(), P(), P(), P(), P()),
        check_vma=False,
    )
```

```python
import functools

import jax
import jax.numpy as jnp
from jax import lax
from jax.experimental import pallas as pl
from jax.experimental.pallas import tpu as pltpu
from jax.sharding import PartitionSpec as P

MIXER_ONE = -2048144789
MIXER_TWO = -1028477387
GOLDEN_STEP = -1640531535
KEEP_LEVEL = 819
KEEP_SCALE = 1024.0 / 819.0
ROOT = 0.7978845608028654
CUBIC = 0.044715
MESH = pl.DeviceIdType.MESH
FLOWS = 3
BF = jnp.bfloat16
F32 = jnp.float32


def shifted(number, places):
    return lax.shift_right_logical(number, jnp.int32(places) if number.ndim == 0 else jnp.full_like(number, places))


def scramble(number):
    number = number ^ shifted(number, 16)
    number = number * jnp.int32(MIXER_ONE)
    number = number ^ shifted(number, 13)
    number = number * jnp.int32(MIXER_TWO)
    return number ^ shifted(number, 16)


def gelu_both(x):
    square = x * x
    t = jnp.tanh(ROOT * (x + CUBIC * (square * x)))
    cdf = 0.5 * (1.0 + t)
    slope = cdf + (0.5 * ROOT) * x * (1.0 - t * t) * (1.0 + (3.0 * CUBIC) * square)
    return x * cdf, slope


def gelu_only(x):
    t = jnp.tanh(ROOT * (x + CUBIC * (x * x * x)))
    return x * (0.5 * (1.0 + t))


def dot(left, right, dims):
    return lax.dot_general(left, right, (dims, ((), ())), preferred_element_type=F32)


NN = ((1,), (0,))
NT = ((1,), (1,))
TN = ((0,), (0,))


def halo_start(xt, top, west, corner, edge, send, recv):
    n_lat = lax.axis_size("lat")
    n_lon = lax.axis_size("lon")
    pipe = lax.axis_index("pipe")
    lat = lax.axis_index("lat")
    lon = lax.axis_index("lon")
    last = xt.shape[0] - 1
    width = xt.shape[2]
    away = n_lon // 2
    is_first = lat == 0
    north = jnp.where(is_first, 0, lat - 1)
    turn = jnp.where(is_first, away, 0)
    has_south = lat < n_lat - 1
    sources = [
        (pipe, lat, (lon + n_lon - 1) % n_lon),
        (pipe, north, (lon + n_lon - turn) % n_lon),
        (pipe, north, (lon + n_lon - turn - 1 + n_lon) % n_lon),
    ]
    barrier = pltpu.get_barrier_semaphore()
    for peer in sources:
        pl.semaphore_signal(barrier, inc=1, device_id=peer, device_id_type=MESH)
    sends = 1 + jnp.where(has_south, 2, 0) + jnp.where(is_first, 2, 0)

    def copy(src, dst, i, j, peer):
        return pltpu.make_async_remote_copy(
            src_ref=src,
            dst_ref=dst,
            send_sem=send.at[i],
            recv_sem=recv.at[j],
            device_id=peer,
            device_id_type=MESH,
        )

    right = pl.ds(width - 128, 128)

    def pair(row, i, lat_to, lon_to):
        return [
            copy(xt.at[row], top, i, 0, (pipe, lat_to, lon_to % n_lon)),
            copy(xt.at[row, :, right], corner, i + 1, 1, (pipe, lat_to, (lon_to + 1) % n_lon)),
        ]

    south = pair(last, 0, jnp.where(has_south, lat + 1, lat), lon)
    pole = pair(0, 2, lat, lon + away)
    pl.semaphore_wait(barrier, sends)

    @pl.when(has_south)
    def _():
        for item in south:
            item.start()

    @pl.when(is_first)
    def _():
        for item in pole:
            item.start()

    row_id = lax.broadcasted_iota(jnp.int32, (128, 128), 0)
    col_id = lax.broadcasted_iota(jnp.int32, (128, 128), 1)
    total = None
    for q in range(last + 1):
        pick = jnp.where((row_id == 127) & (col_id == q), 1.0, 0.0).astype(BF)
        term = dot(xt[q, :, width - 128 :], pick, NN)
        total = term if total is None else total + term
    edge[...] = total.astype(BF)
    east = copy(edge, west, 4, 2, (pipe, lat, (lon + 1) % n_lon))
    east.start()
    def finish():
        for item in pole:
            item.wait_recv()
        east.wait()

        @pl.when(has_south)
        def _():
            for item in south:
                item.wait_send()

        @pl.when(is_first)
        def _():
            for item in pole:
                item.wait_send()

    return finish


def compute_kernel(
    rows,
    cols,
    total_rows,
    scale,
    key_ref,
    xt,
    cw,
    ew,
    pw,
    bias_ref,
    cot,
    field_out,
    payload,
    patches,
    enc_s,
    act_s,
    cot_s,
    di_s,
    dp_s,
    top,
    west,
    corner,
    edge_s,
    send,
    recv,
):
    channels, taps = cw.shape
    hidden = ew.shape[1]
    cells = rows * cols
    pad_taps = patches.shape[0]
    is_encoder = lax.axis_index("pipe") == 0
    lon_cols = cols * lax.axis_size("lon")
    row_base = lax.axis_index("lat") * rows
    col_base = lax.axis_index("lon") * cols

    halo_finish = halo_start(xt, top, west, corner, edge_s, send, recv)

    def selector(first, count):
        shape = (2 * cols, count * cols)
        source = lax.broadcasted_iota(jnp.int32, shape, 0)
        target = lax.broadcasted_iota(jnp.int32, shape, 1)
        tap = target // cols
        wanted = 2 * (target - tap * cols) + tap + first - 1
        return jnp.where(source == wanted, 1.0, 0.0).astype(BF)

    def put(q, b, part):
        places = [(1, q // 2)] if q % 2 else [(a, q // 2 - a // 2) for a in (0, 2)]
        for a, r in places:
            if 0 <= r < rows:
                start = (3 * a + b) * channels
                patches[start : start + channels, r * cols : (r + 1) * cols] = part

    def put_pair(q, line):
        split = dot(line, pair, NN).astype(BF)
        put(q, 1, split[:, :cols])
        put(q, 2, split[:, cols:])

    pair = selector(1, 2)
    for q in range(1, 2 * rows + 1):
        put_pair(q, xt[q - 1])
    edge_row = lax.broadcasted_iota(jnp.int32, (128, cols), 0)
    edge_col = lax.broadcasted_iota(jnp.int32, (128, cols), 1)
    single = selector(0, 1)
    halo_finish()
    put_pair(0, top[...])
    for q in range(2 * rows + 1):
        line = top[...] if q == 0 else xt[q - 1]
        lane = 127 if q == 0 else q - 1
        edge = corner[...] if q == 0 else west[...]
        pick = jnp.where((edge_row == lane) & (edge_col == 0), 1.0, 0.0).astype(BF)
        put(q, 0, (dot(line, single, NN) + dot(edge, pick, NN)).astype(BF))
    patches[taps:, :] = jnp.zeros((pad_taps - taps, cells), BF)

    lanes = lax.broadcasted_iota(jnp.int32, (channels, 128), 1)
    salt = scramble(key_ref[0] + scramble(key_ref[1]))
    step = 2 * cols
    sums = [0.0, 0.0, 0.0]
    for j in range(cells // step):
        here = slice(j * step, (j + 1) * step)
        lane = lax.broadcasted_iota(jnp.int32, (1, step), 1)
        local_row = lane // cols
        cell = (row_base + 2 * j + local_row) * lon_cols + col_base + lane - local_row * cols
        hashed = scramble(cell * jnp.int32(GOLDEN_STEP) + salt)
        bucket = jnp.bitwise_and(shifted(hashed, 8), jnp.int32(1023))
        keep = jnp.where(bucket < KEEP_LEVEL, F32(KEEP_SCALE), F32(0.0))
        pre = dot(cw[...], patches[:taps, here], NN) + bias_ref[:channels]
        value, pre_slope = gelu_both(pre)
        encoded = (value * keep).astype(BF)
        inner = dot(ew[...], encoded, TN) + bias_ref[channels : channels + hidden]
        activated, slope = gelu_both(inner)
        activated = activated.astype(BF)
        scaled = jnp.concatenate([cot[2 * j], cot[2 * j + 1]], axis=1).astype(F32) * scale
        cot_half = scaled.astype(BF)
        d_inner = dot(pw[...], cot_half, TN) * slope
        d_half = d_inner.astype(BF)

        def encoder_part(sums=sums):
            field_out[2 * j] = encoded[:, :cols]
            field_out[2 * j + 1] = encoded[:, cols:]
            d_encoded = (scaled + dot(ew[...], d_half, NN)).astype(BF)
            d_pre = d_encoded.astype(F32) * keep * pre_slope
            dp_s[:, here] = d_pre.astype(BF)
            act_s[0:channels, j * 128 : j * 128 + 128] = jnp.sum(d_pre, axis=1, keepdims=True) + jnp.zeros(
                (channels, 128), F32
            )

        def processor_part():
            processed = (encoded.astype(F32) + dot(pw[...], activated, NN) + bias_ref[channels + hidden :]).astype(BF)
            field_out[2 * j] = processed[:, :cols]
            field_out[2 * j + 1] = processed[:, cols:]
            enc_s[:, here] = encoded
            cot_s[:, here] = cot_half
            di_s[:hidden, here] = activated
            di_s[hidden:, here] = d_half
            bias = jnp.where(lanes == 0, jnp.sum(scaled, axis=1, keepdims=True), 0.0)
            total = jnp.sum(d_inner, axis=1, keepdims=True)
            for k in range(hidden // channels):
                bias = jnp.where(lanes == k + 1, total[k * channels : (k + 1) * channels], bias)
            act_s[0:channels, j * 128 : j * 128 + 128] = bias

        pl.when(is_encoder)(encoder_part)
        pl.when(jnp.logical_not(is_encoder))(processor_part)

    def bias_total():
        total = act_s[:, 0:128]
        for j in range(1, cells // step):
            total = total + act_s[:, j * 128 : j * 128 + 128]
        return total

    blocks = pad_taps // 128

    @pl.when(is_encoder)
    def _():
        for k in range(blocks):
            block = dot(dp_s[...], patches[k * 128 : (k + 1) * 128, :], NT)
            if k == blocks - 1:
                block = jnp.where(lanes == taps - k * 128, bias_total(), block)
            payload[k * channels : (k + 1) * channels, :] = block.astype(BF)

    @pl.when(jnp.logical_not(is_encoder))
    def _():
        per = hidden // 128
        for k in range(per):
            block = dot(cot_s[...], di_s[k * 128 : (k + 1) * 128, :], NT)
            payload[k * channels : (k + 1) * channels, :] = block.astype(BF)
        for k in range(per):
            block = dot(enc_s[...], di_s[hidden + k * 128 : hidden + (k + 1) * 128, :], NT)
            payload[(per + k) * channels : (per + k + 1) * channels, :] = block.astype(BF)
        payload[2 * per * channels : (2 * per + 1) * channels, :] = bias_total().astype(BF)
        rest = (2 * per + 1) * channels
        payload[rest : blocks * channels, :] = jnp.zeros((blocks * channels - rest, 128), BF)

    payload[blocks * channels :, :] = jnp.zeros((total_rows - blocks * channels, 128), BF)


def finish_kernel(taps, hidden, gathered, conv, project, expand, conv_bias, project_bias, expand_bias):
    channels = conv.shape[0]
    blocks = -(-(taps + 1) // 128)
    per = hidden // 128
    for k in range(blocks):
        width = min(128, taps - 128 * k)
        block = gathered[0, k * channels : (k + 1) * channels, :]
        conv[:, 128 * k : 128 * k + width] = block[:, :width].astype(F32)
        if k == blocks - 1:
            pick = lax.broadcasted_iota(jnp.int32, (8, 128), 1) == taps - 128 * k
            conv_bias[...] = dot(jnp.where(pick, 1.0, 0.0).astype(BF), block, NT)[:1]
    for k in range(per):
        here = slice(128 * k, 128 * k + 128)
        project[:, here] = gathered[1, k * channels : (k + 1) * channels, :].astype(F32)
        expand[:, here] = gathered[1, (per + k) * channels : (per + k + 1) * channels, :].astype(F32)
    block = gathered[1, 2 * per * channels : (2 * per + 1) * channels, :]
    pick = lax.broadcasted_iota(jnp.int32, (8, 128), 1) == lax.broadcasted_iota(jnp.int32, (8, 128), 0)
    lines = dot(jnp.where(pick, 1.0, 0.0).astype(BF), block, NT)
    project_bias[...] = lines[:1]
    for k in range(hidden // channels):
        expand_bias[:, k * channels : (k + 1) * channels] = lines[k + 1 : k + 2]


def reduce_kernel(n_x, n_z, flows, payload, out, buf1, s1, buf2, s2, buf3, send, recv):
    pipe = lax.axis_index("pipe")
    lat = lax.axis_index("lat")
    z = lax.axis_index("lon")
    x = lat // 2
    core = lat % 2
    twin = (pipe, 2 * x + 1 - core, z)

    def z_peer(d):
        return (pipe, lat, (z + d) % n_z)

    def xp_peer(dx, dp):
        return ((pipe + dp) % 2, 2 * ((x + dx) % n_x) + core, z)

    others = [(dx, dp) for dp in range(2) for dx in range(n_x) if dx or dp]
    peers = [twin] + [z_peer(d) for d in range(1, n_z)] + [xp_peer(*o) for o in others]
    barrier = pltpu.get_barrier_semaphore()
    for peer in peers:
        pl.semaphore_signal(barrier, inc=1, device_id=peer, device_id_type=MESH)
    pl.semaphore_wait(barrier, len(peers))

    count = [0]
    started = []

    def push(src, dst, peer):
        i = count[0]
        count[0] += 1
        copy = pltpu.make_async_remote_copy(
            src_ref=src,
            dst_ref=dst,
            send_sem=send.at[i],
            recv_sem=recv.at[i],
            device_id=peer,
            device_id_type=MESH,
        )
        copy.start()
        started.append(copy)
        return copy

    def at(start, size):
        return pl.ds(pl.multiple_of(start, 16), size)

    halves = [size // 2 for _, size in flows]
    parts = [half // n_x for half in halves]
    owns = [part // n_z for part in parts]
    ids = range(len(flows))

    firsts = []
    for f in ids:
        start = flows[f][0]
        half = halves[f]
        source = payload.at[at(start + (1 - core) * half, half)]
        firsts.append(push(source, buf1.at[f, pl.ds(0, half)], twin))

    seconds = []
    for f in ids:
        half, part = halves[f], parts[f]
        firsts[f].wait_recv()
        kept = payload[at(flows[f][0] + core * half, half), :]
        s1[f, :half] = (kept.astype(F32) + buf1[f, :half].astype(F32)).astype(BF)
        seconds.append(
            [
                push(
                    s1.at[f, at(((x + d) % n_x) * part, part)],
                    buf2.at[f, d - 1, pl.ds(0, part)],
                    xp_peer(d, 0),
                )
                for d in range(1, n_x)
            ]
        )

    thirds = []
    for f in ids:
        part, own = parts[f], owns[f]
        total = s1[f, at(x * part, part), :].astype(F32)
        for d in range(1, n_x):
            seconds[f][d - 1].wait_recv()
            total = total + buf2[f, d - 1, :part].astype(F32)
        s2[f, :part] = total.astype(BF)
        thirds.append(
            [
                push(
                    s2.at[f, at(((z + d) % n_z) * own, own)],
                    buf3.at[f, d - 1, pl.ds(0, own)],
                    z_peer(d),
                )
                for d in range(1, n_z)
            ]
        )

    fourths = []
    for f in ids:
        part, own = parts[f], owns[f]
        total = s2[f, at(z * own, own), :].astype(F32)
        for d in range(1, n_z):
            thirds[f][d - 1].wait_recv()
            total = total + buf3[f, d - 1, :own].astype(F32)
        place = at(flows[f][0] + core * halves[f] + x * part + z * own, own)
        mine = out.at[pipe, place]
        mine[...] = total.astype(BF)
        fourths.append([push(mine, mine, z_peer(d)) for d in range(1, n_z)])

    fifths = []
    final = []
    for f in ids:
        for copy in fourths[f]:
            copy.wait_recv()
        column = out.at[pipe, at(flows[f][0] + core * halves[f] + x * parts[f], parts[f])]
        fifths.append([push(column, column, xp_peer(*o)) for o in others])
        final.append(push(column, column, twin))
    for f in ids:
        for (dx, dp), copy in zip(others, fifths[f]):
            copy.wait_recv()
            start = flows[f][0] + core * halves[f] + ((x - dx + n_x) % n_x) * parts[f]
            block = out.at[(pipe + dp) % 2, at(start, parts[f])]
            final.append(push(block, block, twin))
    for copy in final:
        copy.wait_recv()
    for copy in started:
        copy.wait_send()


def per_device(
    field,
    conv_weight,
    conv_bias,
    expand_weight,
    expand_bias,
    project_weight,
    project_bias,
    out_cotangent,
    dropout_key,
):
    channels, row_count, col_count = field.shape
    hidden = expand_weight.shape[0]
    taps = conv_weight.shape[1]
    rows = row_count // 2
    cols = col_count // 2
    cells = rows * cols
    n_lat = lax.axis_size("lat")
    n_lon = lax.axis_size("lon")
    scale = float(cells * n_lat * n_lon) ** (-0.5)

    pad_taps = -(-(taps + 1) // 128) * 128
    blocks = pad_taps // 128
    unit = 16 * n_lat * n_lon
    total_rows = -(-(blocks * channels) // unit) * unit
    vmem = pl.BlockSpec(memory_space=pltpu.VMEM)
    smem = pl.BlockSpec(memory_space=pltpu.SMEM)
    turned = jnp.transpose(field, (1, 0, 2))
    field_out, payload = pl.pallas_call(
        functools.partial(compute_kernel, rows, cols, total_rows, scale),
        out_shape=(
            jax.ShapeDtypeStruct((rows, channels, cols), BF),
            jax.ShapeDtypeStruct((total_rows, 128), BF),
        ),
        in_specs=[smem] + [vmem] * 6,
        out_specs=(vmem, vmem),
        scratch_shapes=[
            pltpu.VMEM((pad_taps, cells), BF),
            pltpu.VMEM((channels, cells), BF),
            pltpu.VMEM((channels, cells // (2 * cols) * 128), F32),
            pltpu.VMEM((channels, cells), BF),
            pltpu.VMEM((2 * hidden, cells), BF),
            pltpu.VMEM((channels, cells), BF),
            pltpu.VMEM((channels, col_count), BF),
            pltpu.VMEM((channels, 128), BF),
            pltpu.VMEM((channels, 128), BF),
            pltpu.VMEM((channels, 128), BF),
            pltpu.SemaphoreType.DMA((5,)),
            pltpu.SemaphoreType.DMA((3,)),
        ],
        compiler_params=pltpu.CompilerParams(
            collective_id=1, has_side_effects=True, vmem_limit_bytes=40 * 1024 * 1024
        ),
        name="segment",
    )(
        dropout_key,
        turned,
        conv_weight,
        expand_weight.T,
        project_weight,
        jnp.concatenate([conv_bias, expand_bias, project_bias])[:, None],
        jnp.transpose(out_cotangent, (1, 0, 2)),
    )

    n_x = n_lat // 2
    units = total_rows // unit
    count = min(FLOWS, units)
    sizes = [(units // count + (1 if f < units % count else 0)) * unit for f in range(count)]
    flows = [(sum(sizes[:f]), sizes[f]) for f in range(count)]
    half = sizes[0] // 2
    part = half // n_x
    own = part // n_lon
    copies = count * (1 + (n_x - 1) + 2 * (n_lon - 1) + 2 * (2 * n_x - 1) + 1)
    gathered = pl.pallas_call(
        functools.partial(reduce_kernel, n_x, n_lon, flows),
        out_shape=jax.ShapeDtypeStruct((2, total_rows, 128), BF),
        in_specs=[vmem],
        out_specs=vmem,
        scratch_shapes=[
            pltpu.VMEM((count, half, 128), BF),
            pltpu.VMEM((count, half, 128), BF),
            pltpu.VMEM((count, n_x - 1, part, 128), BF),
            pltpu.VMEM((count, part, 128), BF),
            pltpu.VMEM((count, n_lon - 1, own, 128), BF),
            pltpu.SemaphoreType.DMA((copies,)),
            pltpu.SemaphoreType.DMA((copies,)),
        ],
        compiler_params=pltpu.CompilerParams(
            collective_id=0, has_side_effects=True, vmem_limit_bytes=40 * 1024 * 1024
        ),
        name="gradient_sum",
    )(payload)

    wide = jax.ShapeDtypeStruct((channels, hidden), F32)
    short = jax.ShapeDtypeStruct((1, channels), F32)
    longer = jax.ShapeDtypeStruct((1, hidden), F32)
    conv_grad, project_grad, expand_turned, conv_row, project_row, expand_row = pl.pallas_call(
        functools.partial(finish_kernel, taps, hidden),
        out_shape=(jax.ShapeDtypeStruct((channels, taps), F32), wide, wide, short, short, longer),
        in_specs=[vmem],
        out_specs=(vmem,) * 6,
        compiler_params=pltpu.CompilerParams(vmem_limit_bytes=32 * 1024 * 1024),
        name="widen",
    )(gathered)
    expand_grad = expand_turned.T
    conv_bias_grad = conv_row[0]
    project_bias_grad = project_row[0]
    expand_bias_grad = expand_row[0]
    section_fields = jnp.transpose(field_out, (1, 0, 2))[None]
    return (
        section_fields,
        conv_grad,
        conv_bias_grad,
        expand_grad,
        expand_bias_grad,
        project_grad,
        project_bias_grad,
    )


def solution(mesh):
    placed = (P(None, "lat", "lon"), P(), P(), P(), P(), P(), P(), P(None, "lat", "lon"), P())
    return jax.shard_map(
        per_device,
        mesh=mesh,
        in_specs=placed,
        out_specs=(P("pipe", None, "lat", "lon"), P(), P(), P(), P(), P(), P()),
        check_vma=False,
    )
```

```python
import functools

import jax
import jax.numpy as jnp
from jax import lax
from jax.experimental import pallas as pl
from jax.experimental.pallas import tpu as pltpu
from jax.sharding import PartitionSpec as P

MIXER_ONE = -2048144789
MIXER_TWO = -1028477387
GOLDEN_STEP = -1640531535
KEEP_LEVEL = 819
KEEP_SCALE = 1024.0 / 819.0
ROOT = 0.7978845608028654
CUBIC = 0.044715
MESH = pl.DeviceIdType.MESH
FLOWS = 4
BF = jnp.bfloat16
F32 = jnp.float32


def shifted(number, places):
    return lax.shift_right_logical(number, jnp.int32(places) if number.ndim == 0 else jnp.full_like(number, places))


def scramble(number):
    number = number ^ shifted(number, 16)
    number = number * jnp.int32(MIXER_ONE)
    number = number ^ shifted(number, 13)
    number = number * jnp.int32(MIXER_TWO)
    return number ^ shifted(number, 16)


def gelu_both(x):
    square = x * x
    t = jnp.tanh(ROOT * (x + CUBIC * (square * x)))
    cdf = 0.5 * (1.0 + t)
    slope = cdf + (0.5 * ROOT) * x * (1.0 - t * t) * (1.0 + (3.0 * CUBIC) * square)
    return x * cdf, slope


def gelu_only(x):
    t = jnp.tanh(ROOT * (x + CUBIC * (x * x * x)))
    return x * (0.5 * (1.0 + t))


def dot(left, right, dims):
    return lax.dot_general(left, right, (dims, ((), ())), preferred_element_type=F32)


NN = ((1,), (0,))
NT = ((1,), (1,))
TN = ((0,), (0,))


def halo_start(peers, xt, top, west, corner, edge, send, recv):
    n_lat = lax.axis_size("lat")
    n_lon = lax.axis_size("lon")
    pipe = lax.axis_index("pipe")
    lat = lax.axis_index("lat")
    lon = lax.axis_index("lon")
    last = xt.shape[0] - 1
    width = xt.shape[2]
    away = n_lon // 2
    is_first = lat == 0
    north = jnp.where(is_first, 0, lat - 1)
    turn = jnp.where(is_first, away, 0)
    has_south = lat < n_lat - 1
    sources = [
        (pipe, lat, (lon + n_lon - 1) % n_lon),
        (pipe, north, (lon + n_lon - turn) % n_lon),
        (pipe, north, (lon + n_lon - turn - 1 + n_lon) % n_lon),
    ]
    barrier = pltpu.get_barrier_semaphore()
    for peer in sources + peers:
        pl.semaphore_signal(barrier, inc=1, device_id=peer, device_id_type=MESH)
    sends = len(peers) + 1 + jnp.where(has_south, 2, 0) + jnp.where(is_first, 2, 0)

    def copy(src, dst, i, j, peer):
        return pltpu.make_async_remote_copy(
            src_ref=src,
            dst_ref=dst,
            send_sem=send.at[i],
            recv_sem=recv.at[j],
            device_id=peer,
            device_id_type=MESH,
        )

    right = pl.ds(width - 128, 128)

    def pair(row, i, lat_to, lon_to):
        return [
            copy(xt.at[row], top, i, 0, (pipe, lat_to, lon_to % n_lon)),
            copy(xt.at[row, :, right], corner, i + 1, 1, (pipe, lat_to, (lon_to + 1) % n_lon)),
        ]

    south = pair(last, 0, jnp.where(has_south, lat + 1, lat), lon)
    pole = pair(0, 2, lat, lon + away)
    pl.semaphore_wait(barrier, sends)

    @pl.when(has_south)
    def _():
        for item in south:
            item.start()

    @pl.when(is_first)
    def _():
        for item in pole:
            item.start()

    row_id = lax.broadcasted_iota(jnp.int32, (128, 128), 0)
    col_id = lax.broadcasted_iota(jnp.int32, (128, 128), 1)
    total = None
    for q in range(last + 1):
        pick = jnp.where((row_id == 127) & (col_id == q), 1.0, 0.0).astype(BF)
        term = dot(xt[q, :, width - 128 :], pick, NN)
        total = term if total is None else total + term
    edge[...] = total.astype(BF)
    east = copy(edge, west, 4, 2, (pipe, lat, (lon + 1) % n_lon))
    east.start()
    def finish():
        for item in pole:
            item.wait_recv()
        east.wait()

        @pl.when(has_south)
        def _():
            for item in south:
                item.wait_send()

        @pl.when(is_first)
        def _():
            for item in pole:
                item.wait_send()

    return finish


def reduce_parts(flows, payload, out, buf1, s1, buf2, s2, buf3, send, recv):
    n_x = lax.axis_size("lat") // 2
    n_z = lax.axis_size("lon")
    pipe = lax.axis_index("pipe")
    lat = lax.axis_index("lat")
    z = lax.axis_index("lon")
    x = lat // 2
    core = lat % 2
    twin = (pipe, 2 * x + 1 - core, z)

    def z_peer(d):
        return (pipe, lat, (z + d) % n_z)

    def xp_peer(dx, dp):
        return ((pipe + dp) % 2, 2 * ((x + dx) % n_x) + core, z)

    others = [(dx, dp) for dp in range(2) for dx in range(n_x) if dx or dp]
    peers = [twin] + [z_peer(d) for d in range(1, n_z)] + [xp_peer(*o) for o in others]
    count = [0]
    started = []

    def push(src, dst, peer):
        i = count[0]
        count[0] += 1
        copy = pltpu.make_async_remote_copy(
            src_ref=src,
            dst_ref=dst,
            send_sem=send.at[i],
            recv_sem=recv.at[i],
            device_id=peer,
            device_id_type=MESH,
        )
        copy.start()
        started.append(copy)
        return copy

    def at(start, size):
        return pl.ds(pl.multiple_of(start, 16), size)

    halves = [size // 2 for _, size in flows]
    parts = [half // n_x for half in halves]
    owns = [part // n_z for part in parts]
    ids = range(len(flows))

    firsts = []

    def begin(f):
        start = flows[f][0]
        half = halves[f]
        source = payload.at[at(start + (1 - core) * half, half)]
        firsts.append(push(source, buf1.at[f, pl.ds(0, half)], twin))

    def complete():
        seconds = []
        for f in ids:
            half, part = halves[f], parts[f]
            firsts[f].wait_recv()
            kept = payload[at(flows[f][0] + core * half, half), :]
            s1[f, :half] = (kept.astype(F32) + buf1[f, :half].astype(F32)).astype(BF)
            seconds.append(
                [
                    push(
                        s1.at[f, at(((x + d) % n_x) * part, part)],
                        buf2.at[f, d - 1, pl.ds(0, part)],
                        xp_peer(d, 0),
                    )
                    for d in range(1, n_x)
                ]
            )

        thirds = []
        for f in ids:
            part, own = parts[f], owns[f]
            total = s1[f, at(x * part, part), :].astype(F32)
            for d in range(1, n_x):
                seconds[f][d - 1].wait_recv()
                total = total + buf2[f, d - 1, :part].astype(F32)
            s2[f, :part] = total.astype(BF)
            thirds.append(
                [
                    push(
                        s2.at[f, at(((z + d) % n_z) * own, own)],
                        buf3.at[f, d - 1, pl.ds(0, own)],
                        z_peer(d),
                    )
                    for d in range(1, n_z)
                ]
            )

        fourths = []
        for f in ids:
            part, own = parts[f], owns[f]
            total = s2[f, at(z * own, own), :].astype(F32)
            for d in range(1, n_z):
                thirds[f][d - 1].wait_recv()
                total = total + buf3[f, d - 1, :own].astype(F32)
            place = at(flows[f][0] + core * halves[f] + x * part + z * own, own)
            mine = out.at[pipe, place]
            mine[...] = total.astype(BF)
            fourths.append([push(mine, mine, z_peer(d)) for d in range(1, n_z)])

        fifths = []
        final = []
        for f in ids:
            for copy in fourths[f]:
                copy.wait_recv()
            column = out.at[pipe, at(flows[f][0] + core * halves[f] + x * parts[f], parts[f])]
            fifths.append([push(column, column, xp_peer(*o)) for o in others])
            final.append(push(column, column, twin))
        for f in ids:
            for (dx, dp), copy in zip(others, fifths[f]):
                copy.wait_recv()
                start = flows[f][0] + core * halves[f] + ((x - dx + n_x) % n_x) * parts[f]
                block = out.at[(pipe + dp) % 2, at(start, parts[f])]
                final.append(push(block, block, twin))
        for copy in final:
            copy.wait_recv()
        for copy in started:
            copy.wait_send()

    return peers, begin, complete


def compute_kernel(
    rows,
    cols,
    total_rows,
    scale,
    flows,
    key_ref,
    xt,
    cw,
    ew,
    pw,
    bias_ref,
    cot,
    field_out,
    out,
    patches,
    enc_s,
    act_s,
    cot_s,
    di_s,
    dp_s,
    top,
    west,
    corner,
    edge_s,
    send,
    recv,
    payload,
    buf1,
    s1,
    buf2,
    s2,
    buf3,
    sum_send,
    sum_recv,
):
    channels, taps = cw.shape
    hidden = ew.shape[1]
    cells = rows * cols
    pad_taps = patches.shape[0]
    is_encoder = lax.axis_index("pipe") == 0
    lon_cols = cols * lax.axis_size("lon")
    row_base = lax.axis_index("lat") * rows
    col_base = lax.axis_index("lon") * cols

    peers, begin, complete = reduce_parts(
        flows, payload, out, buf1, s1, buf2, s2, buf3, sum_send, sum_recv
    )
    halo_finish = halo_start(peers, xt, top, west, corner, edge_s, send, recv)

    def selector(first, count):
        shape = (2 * cols, count * cols)
        source = lax.broadcasted_iota(jnp.int32, shape, 0)
        target = lax.broadcasted_iota(jnp.int32, shape, 1)
        tap = target // cols
        wanted = 2 * (target - tap * cols) + tap + first - 1
        return jnp.where(source == wanted, 1.0, 0.0).astype(BF)

    def put(q, b, part):
        places = [(1, q // 2)] if q % 2 else [(a, q // 2 - a // 2) for a in (0, 2)]
        for a, r in places:
            if 0 <= r < rows:
                start = (3 * a + b) * channels
                patches[start : start + channels, r * cols : (r + 1) * cols] = part

    def put_pair(q, line):
        split = dot(line, pair, NN).astype(BF)
        put(q, 1, split[:, :cols])
        put(q, 2, split[:, cols:])

    pair = selector(1, 2)
    for q in range(1, 2 * rows + 1):
        put_pair(q, xt[q - 1])
    edge_row = lax.broadcasted_iota(jnp.int32, (128, cols), 0)
    edge_col = lax.broadcasted_iota(jnp.int32, (128, cols), 1)
    single = selector(0, 1)
    halo_finish()
    put_pair(0, top[...])
    for q in range(2 * rows + 1):
        line = top[...] if q == 0 else xt[q - 1]
        lane = 127 if q == 0 else q - 1
        edge = corner[...] if q == 0 else west[...]
        pick = jnp.where((edge_row == lane) & (edge_col == 0), 1.0, 0.0).astype(BF)
        put(q, 0, (dot(line, single, NN) + dot(edge, pick, NN)).astype(BF))
    patches[taps:, :] = jnp.zeros((pad_taps - taps, cells), BF)

    lanes = lax.broadcasted_iota(jnp.int32, (channels, 128), 1)
    salt = scramble(key_ref[0] + scramble(key_ref[1]))
    step = 2 * cols
    sums = [0.0, 0.0, 0.0]
    for j in range(cells // step):
        here = slice(j * step, (j + 1) * step)
        lane = lax.broadcasted_iota(jnp.int32, (1, step), 1)
        local_row = lane // cols
        cell = (row_base + 2 * j + local_row) * lon_cols + col_base + lane - local_row * cols
        hashed = scramble(cell * jnp.int32(GOLDEN_STEP) + salt)
        bucket = jnp.bitwise_and(shifted(hashed, 8), jnp.int32(1023))
        keep = jnp.where(bucket < KEEP_LEVEL, F32(KEEP_SCALE), F32(0.0))
        pre = dot(cw[...], patches[:taps, here], NN) + bias_ref[:channels]
        value, pre_slope = gelu_both(pre)
        encoded = (value * keep).astype(BF)
        inner = dot(ew[...], encoded, TN) + bias_ref[channels : channels + hidden]
        activated, slope = gelu_both(inner)
        activated = activated.astype(BF)
        scaled = jnp.concatenate([cot[2 * j], cot[2 * j + 1]], axis=1).astype(F32) * scale
        cot_half = scaled.astype(BF)
        d_inner = dot(pw[...], cot_half, TN) * slope
        d_half = d_inner.astype(BF)

        def encoder_part(sums=sums):
            field_out[2 * j] = encoded[:, :cols]
            field_out[2 * j + 1] = encoded[:, cols:]
            d_encoded = (scaled + dot(ew[...], d_half, NN)).astype(BF)
            d_pre = d_encoded.astype(F32) * keep * pre_slope
            dp_s[:, here] = d_pre.astype(BF)
            act_s[0:channels, j * 128 : j * 128 + 128] = jnp.sum(d_pre, axis=1, keepdims=True) + jnp.zeros(
                (channels, 128), F32
            )

        def processor_part():
            processed = (encoded.astype(F32) + dot(pw[...], activated, NN) + bias_ref[channels + hidden :]).astype(BF)
            field_out[2 * j] = processed[:, :cols]
            field_out[2 * j + 1] = processed[:, cols:]
            enc_s[:, here] = encoded
            cot_s[:, here] = cot_half
            di_s[:hidden, here] = activated
            di_s[hidden:, here] = d_half
            bias = jnp.where(lanes == 0, jnp.sum(scaled, axis=1, keepdims=True), 0.0)
            total = jnp.sum(d_inner, axis=1, keepdims=True)
            for k in range(hidden // channels):
                bias = jnp.where(lanes == k + 1, total[k * channels : (k + 1) * channels], bias)
            act_s[0:channels, j * 128 : j * 128 + 128] = bias

        pl.when(is_encoder)(encoder_part)
        pl.when(jnp.logical_not(is_encoder))(processor_part)

    def bias_total():
        total = act_s[:, 0:128]
        for j in range(1, cells // step):
            total = total + act_s[:, j * 128 : j * 128 + 128]
        return total

    blocks = pad_taps // 128

    per = hidden // 128

    def encoder_block(k):
        here = slice(k * channels, (k + 1) * channels)
        block = dot(dp_s[...], patches[k * 128 : (k + 1) * 128, :], NT)
        if k == blocks - 1:
            block = jnp.where(lanes == taps - k * 128, bias_total(), block)
        payload[here, :] = block.astype(BF)

    def processor_block(k):
        here = slice(k * channels, (k + 1) * channels)
        if k < 2 * per:
            left = cot_s if k < per else enc_s
            block = dot(left[...], di_s[k * 128 : (k + 1) * 128, :], NT)
        elif k == 2 * per:
            block = bias_total()
        else:
            block = jnp.zeros((channels, 128), F32)
        payload[here, :] = block.astype(BF)

    payload[blocks * channels :, :] = jnp.zeros((total_rows - blocks * channels, 128), BF)
    done = 0
    for f, (start, size) in enumerate(flows):
        upto = min(blocks, -(-(start + size) // channels))
        todo = range(done, upto)
        done = upto

        @pl.when(is_encoder)
        def _(todo=todo):
            for k in todo:
                encoder_block(k)

        @pl.when(jnp.logical_not(is_encoder))
        def _(todo=todo):
            for k in todo:
                processor_block(k)

        begin(f)
    complete()


def finish_kernel(taps, hidden, gathered, conv, project, expand, conv_bias, project_bias, expand_bias):
    channels = conv.shape[0]
    blocks = -(-(taps + 1) // 128)
    per = hidden // 128
    for k in range(blocks):
        width = min(128, taps - 128 * k)
        block = gathered[0, k * channels : (k + 1) * channels, :]
        conv[:, 128 * k : 128 * k + width] = block[:, :width].astype(F32)
        if k == blocks - 1:
            pick = lax.broadcasted_iota(jnp.int32, (8, 128), 1) == taps - 128 * k
            conv_bias[...] = dot(jnp.where(pick, 1.0, 0.0).astype(BF), block, NT)[:1]
    for k in range(per):
        here = slice(128 * k, 128 * k + 128)
        project[:, here] = gathered[1, k * channels : (k + 1) * channels, :].astype(F32)
        expand[:, here] = gathered[1, (per + k) * channels : (per + k + 1) * channels, :].astype(F32)
    block = gathered[1, 2 * per * channels : (2 * per + 1) * channels, :]
    pick = lax.broadcasted_iota(jnp.int32, (8, 128), 1) == lax.broadcasted_iota(jnp.int32, (8, 128), 0)
    lines = dot(jnp.where(pick, 1.0, 0.0).astype(BF), block, NT)
    project_bias[...] = lines[:1]
    for k in range(hidden // channels):
        expand_bias[:, k * channels : (k + 1) * channels] = lines[k + 1 : k + 2]


def per_device(
    field,
    conv_weight,
    conv_bias,
    expand_weight,
    expand_bias,
    project_weight,
    project_bias,
    out_cotangent,
    dropout_key,
):
    channels, row_count, col_count = field.shape
    hidden = expand_weight.shape[0]
    taps = conv_weight.shape[1]
    rows = row_count // 2
    cols = col_count // 2
    cells = rows * cols
    n_lat = lax.axis_size("lat")
    n_lon = lax.axis_size("lon")
    scale = float(cells * n_lat * n_lon) ** (-0.5)

    pad_taps = -(-(taps + 1) // 128) * 128
    blocks = pad_taps // 128
    unit = 16 * n_lat * n_lon
    total_rows = -(-(blocks * channels) // unit) * unit
    vmem = pl.BlockSpec(memory_space=pltpu.VMEM)
    smem = pl.BlockSpec(memory_space=pltpu.SMEM)
    n_x = n_lat // 2
    units = total_rows // unit
    count = min(FLOWS, units)
    sizes = [(units // count + (1 if f < units % count else 0)) * unit for f in range(count)]
    flows = [(sum(sizes[:f]), sizes[f]) for f in range(count)]
    half = sizes[0] // 2
    part = half // n_x
    own = part // n_lon
    copies = count * (1 + (n_x - 1) + 2 * (n_lon - 1) + 2 * (2 * n_x - 1) + 1)
    turned = jnp.transpose(field, (1, 0, 2))
    field_out, gathered = pl.pallas_call(
        functools.partial(compute_kernel, rows, cols, total_rows, scale, flows),
        out_shape=(
            jax.ShapeDtypeStruct((rows, channels, cols), BF),
            jax.ShapeDtypeStruct((2, total_rows, 128), BF),
        ),
        in_specs=[smem] + [vmem] * 6,
        out_specs=(vmem, vmem),
        scratch_shapes=[
            pltpu.VMEM((pad_taps, cells), BF),
            pltpu.VMEM((channels, cells), BF),
            pltpu.VMEM((channels, cells // (2 * cols) * 128), F32),
            pltpu.VMEM((channels, cells), BF),
            pltpu.VMEM((2 * hidden, cells), BF),
            pltpu.VMEM((channels, cells), BF),
            pltpu.VMEM((channels, col_count), BF),
            pltpu.VMEM((channels, 128), BF),
            pltpu.VMEM((channels, 128), BF),
            pltpu.VMEM((channels, 128), BF),
            pltpu.SemaphoreType.DMA((5,)),
            pltpu.SemaphoreType.DMA((3,)),
            pltpu.VMEM((total_rows, 128), BF),
            pltpu.VMEM((count, half, 128), BF),
            pltpu.VMEM((count, half, 128), BF),
            pltpu.VMEM((count, n_x - 1, part, 128), BF),
            pltpu.VMEM((count, part, 128), BF),
            pltpu.VMEM((count, n_lon - 1, own, 128), BF),
            pltpu.SemaphoreType.DMA((copies,)),
            pltpu.SemaphoreType.DMA((copies,)),
        ],
        compiler_params=pltpu.CompilerParams(
            collective_id=1, has_side_effects=True, vmem_limit_bytes=40 * 1024 * 1024
        ),
        name="segment",
    )(
        dropout_key,
        turned,
        conv_weight,
        expand_weight.T,
        project_weight,
        jnp.concatenate([conv_bias, expand_bias, project_bias])[:, None],
        jnp.transpose(out_cotangent, (1, 0, 2)),
    )

    wide = jax.ShapeDtypeStruct((channels, hidden), F32)
    short = jax.ShapeDtypeStruct((1, channels), F32)
    longer = jax.ShapeDtypeStruct((1, hidden), F32)
    conv_grad, project_grad, expand_turned, conv_row, project_row, expand_row = pl.pallas_call(
        functools.partial(finish_kernel, taps, hidden),
        out_shape=(jax.ShapeDtypeStruct((channels, taps), F32), wide, wide, short, short, longer),
        in_specs=[vmem],
        out_specs=(vmem,) * 6,
        compiler_params=pltpu.CompilerParams(vmem_limit_bytes=32 * 1024 * 1024),
        name="widen",
    )(gathered)
    expand_grad = expand_turned.T
    conv_bias_grad = conv_row[0]
    project_bias_grad = project_row[0]
    expand_bias_grad = expand_row[0]
    section_fields = jnp.transpose(field_out, (1, 0, 2))[None]
    return (
        section_fields,
        conv_grad,
        conv_bias_grad,
        expand_grad,
        expand_bias_grad,
        project_grad,
        project_bias_grad,
    )


def solution(mesh):
    placed = (P(None, "lat", "lon"), P(), P(), P(), P(), P(), P(), P(None, "lat", "lon"), P())
    return jax.shard_map(
        per_device,
        mesh=mesh,
        in_specs=placed,
        out_specs=(P("pipe", None, "lat", "lon"), P(), P(), P(), P(), P(), P()),
        check_vma=False,
    )
```

```python
import functools

import jax
import jax.numpy as jnp
from jax import lax
from jax.experimental import pallas as pl
from jax.experimental.pallas import tpu as pltpu
from jax.sharding import PartitionSpec as P

MIXER_ONE = -2048144789
MIXER_TWO = -1028477387
GOLDEN_STEP = -1640531535
KEEP_LEVEL = 819
KEEP_SCALE = 1024.0 / 819.0
ROOT = 0.7978845608028654
CUBIC = 0.044715
MESH = pl.DeviceIdType.MESH
FLOWS = 4
BF = jnp.bfloat16
F32 = jnp.float32


def shifted(number, places):
    return lax.shift_right_logical(number, jnp.int32(places) if number.ndim == 0 else jnp.full_like(number, places))


def scramble(number):
    number = number ^ shifted(number, 16)
    number = number * jnp.int32(MIXER_ONE)
    number = number ^ shifted(number, 13)
    number = number * jnp.int32(MIXER_TWO)
    return number ^ shifted(number, 16)


def gelu_both(x):
    square = x * x
    t = jnp.tanh(ROOT * (x + CUBIC * (square * x)))
    cdf = 0.5 * (1.0 + t)
    slope = cdf + (0.5 * ROOT) * x * (1.0 - t * t) * (1.0 + (3.0 * CUBIC) * square)
    return x * cdf, slope


def gelu_only(x):
    t = jnp.tanh(ROOT * (x + CUBIC * (x * x * x)))
    return x * (0.5 * (1.0 + t))


def dot(left, right, dims):
    return lax.dot_general(left, right, (dims, ((), ())), preferred_element_type=F32)


NN = ((1,), (0,))
NT = ((1,), (1,))
TN = ((0,), (0,))


def halo_start(peers, xt, top, west, corner, edge, send, recv):
    n_lat = lax.axis_size("lat")
    n_lon = lax.axis_size("lon")
    pipe = lax.axis_index("pipe")
    lat = lax.axis_index("lat")
    lon = lax.axis_index("lon")
    last = xt.shape[0] - 1
    width = xt.shape[2]
    away = n_lon // 2
    is_first = lat == 0
    north = jnp.where(is_first, 0, lat - 1)
    turn = jnp.where(is_first, away, 0)
    has_south = lat < n_lat - 1
    sources = [
        (pipe, lat, (lon + n_lon - 1) % n_lon),
        (pipe, north, (lon + n_lon - turn) % n_lon),
        (pipe, north, (lon + n_lon - turn - 1 + n_lon) % n_lon),
    ]
    barrier = pltpu.get_barrier_semaphore()
    for peer in sources + peers:
        pl.semaphore_signal(barrier, inc=1, device_id=peer, device_id_type=MESH)
    sends = len(peers) + 1 + jnp.where(has_south, 2, 0) + jnp.where(is_first, 2, 0)

    def copy(src, dst, i, j, peer):
        return pltpu.make_async_remote_copy(
            src_ref=src,
            dst_ref=dst,
            send_sem=send.at[i],
            recv_sem=recv.at[j],
            device_id=peer,
            device_id_type=MESH,
        )

    right = pl.ds(width - 128, 128)

    def pair(row, i, lat_to, lon_to):
        return [
            copy(xt.at[row], top, i, 0, (pipe, lat_to, lon_to % n_lon)),
            copy(xt.at[row, :, right], corner, i + 1, 1, (pipe, lat_to, (lon_to + 1) % n_lon)),
        ]

    south = pair(last, 0, jnp.where(has_south, lat + 1, lat), lon)
    pole = pair(0, 2, lat, lon + away)
    pl.semaphore_wait(barrier, sends)

    @pl.when(has_south)
    def _():
        for item in south:
            item.start()

    @pl.when(is_first)
    def _():
        for item in pole:
            item.start()

    row_id = lax.broadcasted_iota(jnp.int32, (128, 128), 0)
    col_id = lax.broadcasted_iota(jnp.int32, (128, 128), 1)
    total = None
    for q in range(last + 1):
        pick = jnp.where((row_id == 127) & (col_id == q), 1.0, 0.0).astype(BF)
        term = dot(xt[q, :, width - 128 :], pick, NN)
        total = term if total is None else total + term
    edge[...] = total.astype(BF)
    east = copy(edge, west, 4, 2, (pipe, lat, (lon + 1) % n_lon))
    east.start()
    def finish():
        for item in pole:
            item.wait_recv()
        east.wait()

        @pl.when(has_south)
        def _():
            for item in south:
                item.wait_send()

        @pl.when(is_first)
        def _():
            for item in pole:
                item.wait_send()

    return finish


def reduce_parts(flows, payload, out, buf1, s1, buf2, s2, buf3, send, recv):
    n_x = lax.axis_size("lat") // 2
    n_z = lax.axis_size("lon")
    pipe = lax.axis_index("pipe")
    lat = lax.axis_index("lat")
    z = lax.axis_index("lon")
    x = lat // 2
    core = lat % 2
    twin = (pipe, 2 * x + 1 - core, z)

    def z_peer(d):
        return (pipe, lat, (z + d) % n_z)

    def xp_peer(dx, dp):
        return ((pipe + dp) % 2, 2 * ((x + dx) % n_x) + core, z)

    others = [(dx, dp) for dp in range(2) for dx in range(n_x) if dx or dp]
    peers = [twin] + [z_peer(d) for d in range(1, n_z)] + [xp_peer(*o) for o in others]
    count = [0]
    started = []

    def push(src, dst, peer):
        i = count[0]
        count[0] += 1
        copy = pltpu.make_async_remote_copy(
            src_ref=src,
            dst_ref=dst,
            send_sem=send.at[i],
            recv_sem=recv.at[i],
            device_id=peer,
            device_id_type=MESH,
        )
        copy.start()
        started.append(copy)
        return copy

    def at(start, size):
        return pl.ds(pl.multiple_of(start, 16), size)

    halves = [size // 2 for _, size in flows]
    parts = [half // n_x for half in halves]
    owns = [part // n_z for part in parts]
    ids = range(len(flows))

    firsts = []

    def begin(f):
        start = flows[f][0]
        half = halves[f]
        source = payload.at[at(start + (1 - core) * half, half)]
        firsts.append(push(source, buf1.at[f, pl.ds(0, half)], twin))

    def complete():
        seconds, thirds, fourths, fifths, final = [], [], [], [], []

        def stage_1(f):
            half, part = halves[f], parts[f]
            firsts[f].wait_recv()
            kept = payload[at(flows[f][0] + core * half, half), :]
            s1[f, :half] = (kept.astype(F32) + buf1[f, :half].astype(F32)).astype(BF)
            seconds.append(
                [
                    push(
                        s1.at[f, at(((x + d) % n_x) * part, part)],
                        buf2.at[f, d - 1, pl.ds(0, part)],
                        xp_peer(d, 0),
                    )
                    for d in range(1, n_x)
                ]
            )

        def stage_2(f):
            part, own = parts[f], owns[f]
            total = s1[f, at(x * part, part), :].astype(F32)
            for d in range(1, n_x):
                seconds[f][d - 1].wait_recv()
                total = total + buf2[f, d - 1, :part].astype(F32)
            s2[f, :part] = total.astype(BF)
            thirds.append(
                [
                    push(
                        s2.at[f, at(((z + d) % n_z) * own, own)],
                        buf3.at[f, d - 1, pl.ds(0, own)],
                        z_peer(d),
                    )
                    for d in range(1, n_z)
                ]
            )

        def stage_3(f):
            part, own = parts[f], owns[f]
            total = s2[f, at(z * own, own), :].astype(F32)
            for d in range(1, n_z):
                thirds[f][d - 1].wait_recv()
                total = total + buf3[f, d - 1, :own].astype(F32)
            place = at(flows[f][0] + core * halves[f] + x * part + z * own, own)
            mine = out.at[pipe, place]
            mine[...] = total.astype(BF)
            fourths.append([push(mine, mine, z_peer(d)) for d in range(1, n_z)])

        def stage_4(f):
            for copy in fourths[f]:
                copy.wait_recv()
            column = out.at[pipe, at(flows[f][0] + core * halves[f] + x * parts[f], parts[f])]
            fifths.append([push(column, column, xp_peer(*o)) for o in others])
            final.append(push(column, column, twin))

        def stage_5(f):
            for (dx, dp), copy in zip(others, fifths[f]):
                copy.wait_recv()
                start = flows[f][0] + core * halves[f] + ((x - dx + n_x) % n_x) * parts[f]
                block = out.at[(pipe + dp) % 2, at(start, parts[f])]
                final.append(push(block, block, twin))

        stages = [stage_1, stage_2, stage_3, stage_4, stage_5]
        for turn in range(len(flows) + len(stages) - 1):
            for f in ids:
                if 0 <= turn - f < len(stages):
                    stages[turn - f](f)
        for copy in final:
            copy.wait_recv()
        for copy in started:
            copy.wait_send()

    return peers, begin, complete


def compute_kernel(
    rows,
    cols,
    total_rows,
    scale,
    flows,
    key_ref,
    xt,
    cw,
    ew,
    pw,
    bias_ref,
    cot,
    field_out,
    out,
    patches,
    enc_s,
    act_s,
    cot_s,
    di_s,
    dp_s,
    top,
    west,
    corner,
    edge_s,
    send,
    recv,
    payload,
    buf1,
    s1,
    buf2,
    s2,
    buf3,
    sum_send,
    sum_recv,
):
    channels, taps = cw.shape
    hidden = ew.shape[1]
    cells = rows * cols
    pad_taps = patches.shape[0]
    is_encoder = lax.axis_index("pipe") == 0
    lon_cols = cols * lax.axis_size("lon")
    row_base = lax.axis_index("lat") * rows
    col_base = lax.axis_index("lon") * cols

    peers, begin, complete = reduce_parts(
        flows, payload, out, buf1, s1, buf2, s2, buf3, sum_send, sum_recv
    )
    halo_finish = halo_start(peers, xt, top, west, corner, edge_s, send, recv)

    def selector(first, count):
        shape = (2 * cols, count * cols)
        source = lax.broadcasted_iota(jnp.int32, shape, 0)
        target = lax.broadcasted_iota(jnp.int32, shape, 1)
        tap = target // cols
        wanted = 2 * (target - tap * cols) + tap + first - 1
        return jnp.where(source == wanted, 1.0, 0.0).astype(BF)

    def put(q, b, part):
        places = [(1, q // 2)] if q % 2 else [(a, q // 2 - a // 2) for a in (0, 2)]
        for a, r in places:
            if 0 <= r < rows:
                start = (3 * a + b) * channels
                patches[start : start + channels, r * cols : (r + 1) * cols] = part

    def put_pair(q, line):
        split = dot(line, pair, NN).astype(BF)
        put(q, 1, split[:, :cols])
        put(q, 2, split[:, cols:])

    pair = selector(1, 2)
    for q in range(1, 2 * rows + 1):
        put_pair(q, xt[q - 1])
    edge_row = lax.broadcasted_iota(jnp.int32, (128, cols), 0)
    edge_col = lax.broadcasted_iota(jnp.int32, (128, cols), 1)
    single = selector(0, 1)
    halo_finish()
    put_pair(0, top[...])
    for q in range(2 * rows + 1):
        line = top[...] if q == 0 else xt[q - 1]
        lane = 127 if q == 0 else q - 1
        edge = corner[...] if q == 0 else west[...]
        pick = jnp.where((edge_row == lane) & (edge_col == 0), 1.0, 0.0).astype(BF)
        put(q, 0, (dot(line, single, NN) + dot(edge, pick, NN)).astype(BF))
    patches[taps:, :] = jnp.zeros((pad_taps - taps, cells), BF)

    lanes = lax.broadcasted_iota(jnp.int32, (channels, 128), 1)
    salt = scramble(key_ref[0] + scramble(key_ref[1]))
    step = 2 * cols
    sums = [0.0, 0.0, 0.0]
    for j in range(cells // step):
        here = slice(j * step, (j + 1) * step)
        lane = lax.broadcasted_iota(jnp.int32, (1, step), 1)
        local_row = lane // cols
        cell = (row_base + 2 * j + local_row) * lon_cols + col_base + lane - local_row * cols
        hashed = scramble(cell * jnp.int32(GOLDEN_STEP) + salt)
        bucket = jnp.bitwise_and(shifted(hashed, 8), jnp.int32(1023))
        keep = jnp.where(bucket < KEEP_LEVEL, F32(KEEP_SCALE), F32(0.0))
        pre = dot(cw[...], patches[:taps, here], NN) + bias_ref[:channels]
        value, pre_slope = gelu_both(pre)
        encoded = (value * keep).astype(BF)
        inner = dot(ew[...], encoded, TN) + bias_ref[channels : channels + hidden]
        activated, slope = gelu_both(inner)
        activated = activated.astype(BF)
        scaled = jnp.concatenate([cot[2 * j], cot[2 * j + 1]], axis=1).astype(F32) * scale
        cot_half = scaled.astype(BF)
        d_inner = dot(pw[...], cot_half, TN) * slope
        d_half = d_inner.astype(BF)

        def encoder_part(sums=sums):
            field_out[2 * j] = encoded[:, :cols]
            field_out[2 * j + 1] = encoded[:, cols:]
            d_encoded = (scaled + dot(ew[...], d_half, NN)).astype(BF)
            d_pre = d_encoded.astype(F32) * keep * pre_slope
            dp_s[:, here] = d_pre.astype(BF)
            act_s[0:channels, j * 128 : j * 128 + 128] = jnp.sum(d_pre, axis=1, keepdims=True) + jnp.zeros(
                (channels, 128), F32
            )

        def processor_part():
            processed = (encoded.astype(F32) + dot(pw[...], activated, NN) + bias_ref[channels + hidden :]).astype(BF)
            field_out[2 * j] = processed[:, :cols]
            field_out[2 * j + 1] = processed[:, cols:]
            enc_s[:, here] = encoded
            cot_s[:, here] = cot_half
            di_s[:hidden, here] = activated
            di_s[hidden:, here] = d_half
            bias = jnp.where(lanes == 0, jnp.sum(scaled, axis=1, keepdims=True), 0.0)
            total = jnp.sum(d_inner, axis=1, keepdims=True)
            for k in range(hidden // channels):
                bias = jnp.where(lanes == k + 1, total[k * channels : (k + 1) * channels], bias)
            act_s[0:channels, j * 128 : j * 128 + 128] = bias

        pl.when(is_encoder)(encoder_part)
        pl.when(jnp.logical_not(is_encoder))(processor_part)

    def bias_total():
        total = act_s[:, 0:128]
        for j in range(1, cells // step):
            total = total + act_s[:, j * 128 : j * 128 + 128]
        return total

    blocks = pad_taps // 128

    per = hidden // 128

    def encoder_block(k):
        here = slice(k * channels, (k + 1) * channels)
        block = dot(dp_s[...], patches[k * 128 : (k + 1) * 128, :], NT)
        if k == blocks - 1:
            block = jnp.where(lanes == taps - k * 128, bias_total(), block)
        payload[here, :] = block.astype(BF)

    def processor_block(k):
        here = slice(k * channels, (k + 1) * channels)
        if k < 2 * per:
            left = cot_s if k < per else enc_s
            block = dot(left[...], di_s[k * 128 : (k + 1) * 128, :], NT)
        elif k == 2 * per:
            block = bias_total()
        else:
            block = jnp.zeros((channels, 128), F32)
        payload[here, :] = block.astype(BF)

    payload[blocks * channels :, :] = jnp.zeros((total_rows - blocks * channels, 128), BF)
    done = 0
    for f, (start, size) in enumerate(flows):
        upto = min(blocks, -(-(start + size) // channels))
        todo = range(done, upto)
        done = upto

        @pl.when(is_encoder)
        def _(todo=todo):
            for k in todo:
                encoder_block(k)

        @pl.when(jnp.logical_not(is_encoder))
        def _(todo=todo):
            for k in todo:
                processor_block(k)

        begin(f)
    complete()


def finish_kernel(taps, hidden, gathered, conv, project, expand, conv_bias, project_bias, expand_bias):
    channels = conv.shape[0]
    blocks = -(-(taps + 1) // 128)
    per = hidden // 128
    for k in range(blocks):
        width = min(128, taps - 128 * k)
        block = gathered[0, k * channels : (k + 1) * channels, :]
        conv[:, 128 * k : 128 * k + width] = block[:, :width].astype(F32)
        if k == blocks - 1:
            pick = lax.broadcasted_iota(jnp.int32, (8, 128), 1) == taps - 128 * k
            conv_bias[...] = dot(jnp.where(pick, 1.0, 0.0).astype(BF), block, NT)[:1]
    for k in range(per):
        here = slice(128 * k, 128 * k + 128)
        project[:, here] = gathered[1, k * channels : (k + 1) * channels, :].astype(F32)
        expand[:, here] = gathered[1, (per + k) * channels : (per + k + 1) * channels, :].astype(F32)
    block = gathered[1, 2 * per * channels : (2 * per + 1) * channels, :]
    pick = lax.broadcasted_iota(jnp.int32, (8, 128), 1) == lax.broadcasted_iota(jnp.int32, (8, 128), 0)
    lines = dot(jnp.where(pick, 1.0, 0.0).astype(BF), block, NT)
    project_bias[...] = lines[:1]
    for k in range(hidden // channels):
        expand_bias[:, k * channels : (k + 1) * channels] = lines[k + 1 : k + 2]


def per_device(
    field,
    conv_weight,
    conv_bias,
    expand_weight,
    expand_bias,
    project_weight,
    project_bias,
    out_cotangent,
    dropout_key,
):
    channels, row_count, col_count = field.shape
    hidden = expand_weight.shape[0]
    taps = conv_weight.shape[1]
    rows = row_count // 2
    cols = col_count // 2
    cells = rows * cols
    n_lat = lax.axis_size("lat")
    n_lon = lax.axis_size("lon")
    scale = float(cells * n_lat * n_lon) ** (-0.5)

    pad_taps = -(-(taps + 1) // 128) * 128
    blocks = pad_taps // 128
    unit = 16 * n_lat * n_lon
    total_rows = -(-(blocks * channels) // unit) * unit
    vmem = pl.BlockSpec(memory_space=pltpu.VMEM)
    smem = pl.BlockSpec(memory_space=pltpu.SMEM)
    n_x = n_lat // 2
    units = total_rows // unit
    count = min(FLOWS, units)
    sizes = [(units // count + (1 if f < units % count else 0)) * unit for f in range(count)]
    flows = [(sum(sizes[:f]), sizes[f]) for f in range(count)]
    half = sizes[0] // 2
    part = half // n_x
    own = part // n_lon
    copies = count * (1 + (n_x - 1) + 2 * (n_lon - 1) + 2 * (2 * n_x - 1) + 1)
    turned = jnp.transpose(field, (1, 0, 2))
    field_out, gathered = pl.pallas_call(
        functools.partial(compute_kernel, rows, cols, total_rows, scale, flows),
        out_shape=(
            jax.ShapeDtypeStruct((rows, channels, cols), BF),
            jax.ShapeDtypeStruct((2, total_rows, 128), BF),
        ),
        in_specs=[smem] + [vmem] * 6,
        out_specs=(vmem, vmem),
        scratch_shapes=[
            pltpu.VMEM((pad_taps, cells), BF),
            pltpu.VMEM((channels, cells), BF),
            pltpu.VMEM((channels, cells // (2 * cols) * 128), F32),
            pltpu.VMEM((channels, cells), BF),
            pltpu.VMEM((2 * hidden, cells), BF),
            pltpu.VMEM((channels, cells), BF),
            pltpu.VMEM((channels, col_count), BF),
            pltpu.VMEM((channels, 128), BF),
            pltpu.VMEM((channels, 128), BF),
            pltpu.VMEM((channels, 128), BF),
            pltpu.SemaphoreType.DMA((5,)),
            pltpu.SemaphoreType.DMA((3,)),
            pltpu.VMEM((total_rows, 128), BF),
            pltpu.VMEM((count, half, 128), BF),
            pltpu.VMEM((count, half, 128), BF),
            pltpu.VMEM((count, n_x - 1, part, 128), BF),
            pltpu.VMEM((count, part, 128), BF),
            pltpu.VMEM((count, n_lon - 1, own, 128), BF),
            pltpu.SemaphoreType.DMA((copies,)),
            pltpu.SemaphoreType.DMA((copies,)),
        ],
        compiler_params=pltpu.CompilerParams(
            collective_id=1, has_side_effects=True, vmem_limit_bytes=40 * 1024 * 1024
        ),
        name="segment",
    )(
        dropout_key,
        turned,
        conv_weight,
        expand_weight.T,
        project_weight,
        jnp.concatenate([conv_bias, expand_bias, project_bias])[:, None],
        jnp.transpose(out_cotangent, (1, 0, 2)),
    )

    wide = jax.ShapeDtypeStruct((channels, hidden), F32)
    short = jax.ShapeDtypeStruct((1, channels), F32)
    longer = jax.ShapeDtypeStruct((1, hidden), F32)
    conv_grad, project_grad, expand_turned, conv_row, project_row, expand_row = pl.pallas_call(
        functools.partial(finish_kernel, taps, hidden),
        out_shape=(jax.ShapeDtypeStruct((channels, taps), F32), wide, wide, short, short, longer),
        in_specs=[vmem],
        out_specs=(vmem,) * 6,
        compiler_params=pltpu.CompilerParams(vmem_limit_bytes=32 * 1024 * 1024),
        name="widen",
    )(gathered)
    expand_grad = expand_turned.T
    conv_bias_grad = conv_row[0]
    project_bias_grad = project_row[0]
    expand_bias_grad = expand_row[0]
    section_fields = jnp.transpose(field_out, (1, 0, 2))[None]
    return (
        section_fields,
        conv_grad,
        conv_bias_grad,
        expand_grad,
        expand_bias_grad,
        project_grad,
        project_bias_grad,
    )


def solution(mesh):
    placed = (P(None, "lat", "lon"), P(), P(), P(), P(), P(), P(), P(None, "lat", "lon"), P())
    return jax.shard_map(
        per_device,
        mesh=mesh,
        in_specs=placed,
        out_specs=(P("pipe", None, "lat", "lon"), P(), P(), P(), P(), P(), P()),
        check_vma=False,
    )
```
